32 devices in a mesh: expert: 16 (over z, y, x), tensor: 1, dp: 2 (over core).
Axes of the slice: x: 2, y: 2, z: 4, core: 2. Of those that a mesh axis runs over, the one named last changes fastest.
Arguments:
- tokens: bfloat16 [2048, 7168], P(('expert', 'dp'), 'tensor'), may hold values from -6 to 6
- gate_weight: bfloat16 [16, 7168, 1024], P('expert', 'tensor', 'dp'), may hold values from -0.25 to 0.25
- up_weight: bfloat16 [16, 7168, 1024], P('expert', 'tensor', 'dp'), may hold values from -0.25 to 0.25
- down_weight: bfloat16 [16, 1024, 7168], P('expert', 'dp', 'tensor'), may hold values from -0.1875 to 0.1875
- sketch: bfloat16 [16, 2, 1024, 512], P('expert', None, 'dp'), may hold values from -6 to 6
- clusters: int32 [16], replicated, may hold values from 0 to 5, never falling along the last dimension, each value on 1 to 4 neighbouring positions
- routes: int32 [2048, 8], P(('expert', 'dp')), may hold values from 0 to 15, all different within a row; in each aligned block of 64 rows (0 to 63, 64 to 127, ...) at most 48 rows name the same one
- route_weights: float32 [2048, 8], P(('expert', 'dp')), may hold values from 0.05 to 0.3
Outputs:
- mixed: bfloat16 [2048, 7168], P(('expert', 'dp'), 'tensor')
The draws below stay inside these ranges and needn't reach their ends.
Inputs may be any that keep to these rules, and one draw needn't show every extreme that they name: `clusters`: the experts of one cluster are consecutive; a cluster holds 1 to 4 experts, and one holds exactly 4. `routes`: A row names 8 different experts. In each aligned block of 64 rows (the rows of one device) no expert is named by more than 48 rows, a bound that some block reaches.
All inputs are finite; a program needn't handle non-finite values.
Results may differ from the reference program's by a relative error of at most 0.023.
Values may be sent and summed in bfloat16 or wider, within the bound.
No kernel may reach another device: no remote copies, remote signals or barrier semaphores. Data moves between devices by JAX's collectives and lax.ppermute only.
A program may use at most 128 MiB of HBM per device.

```python
import math
import jax
import jax.numpy as jnp
import numpy as np
from jax import lax

D = 7168
HID = 1024
RANK = 512
TOP = 8
MOST = 4
TOK_DEV = 64
EXPERTS = 16
CLUSTERS = 6
CAP = 48
TOKENS = 2048
N_EXPERT = 16
N_TENSOR = 1
N_DP = 2


def shard_levels(rng, dims, split, low, high):
    def one(dim, parts):
        heights = jax.random.uniform(jax.random.fold_in(jax.random.fold_in(rng, 6), dim), (parts,), jnp.float32, low / len(split), high / len(split))
        return jnp.repeat(jnp.exp(heights), dims[dim] // parts).reshape((-1,) + (1,) * (len(dims) - dim - 1))

    factor_of = one(*split[0])
    for cut in split[1:]:
        factor_of = factor_of * one(*cut)
    return factor_of


def length_profile(count, total, reach, slope):
    portions = [(1 << 20) // math.isqrt(standing ** slope) + 1 for standing in range(2, count + 1)]
    spare, counts = total - reach - (count - 1), [1] * (count - 1)
    while spare > 0:
        free = [i for i in range(count - 1) if counts[i] < reach]
        pool, remaining = sum([portions[i] for i in free]), spare
        for i in free:
            more = min(reach - counts[i], max(1, remaining * portions[i] // pool), spare)
            counts[i] = counts[i] + more
            spare = spare - more
    return np.array([reach] + counts)


def uneven(rng, amount, total, limit, lean):
    if amount == 2:
        one = jax.random.randint(rng, (), max(1, total - limit), min(limit, total - 1) + 1)
        return jnp.stack([one, total - one])
    lengths = jnp.asarray(length_profile(amount, total, limit, lean), jnp.int32)
    couples = (amount - 1) // 2
    giver, receiver = lengths[1:1 + 2 * couples:2], lengths[2:2 + 2 * couples:2]
    room = jnp.minimum(giver - 1, limit - receiver)
    shifted = jax.random.randint(jax.random.fold_in(rng, 1), (couples,), 0, 1 << 20) % (room + 1)
    lengths = lengths.at[1:1 + 2 * couples:2].set(giver - shifted).at[2:2 + 2 * couples:2].set(receiver + shifted)
    return lengths[jax.random.permutation(jax.random.fold_in(rng, 2), amount)]


def routed_block(stream_key, own, number, rows, amount, top, bound, lean):
    ranking = jax.random.permutation(stream_key, amount)
    heavy_load, common = portions_of(amount, rows * top, bound, lean, True), portions_of(amount, rows * top, bound, lean, False)
    places = jnp.arange(amount)

    def named(lengths, offset_by):
        used = int((lengths > 0).sum())
        fixed = max(1, used // 4)
        passed = fixed + (places - fixed + offset_by * (used - fixed)) % max(1, amount - fixed)
        return jnp.zeros((amount,), jnp.int32).at[ranking[jnp.where(places < fixed, places, passed)]].set(jnp.asarray(lengths, jnp.int32))

    lengths = jnp.where(number % 4 == 0, named(heavy_load, number // 4), named(common, number - number // 4 - 1))
    mixed = jax.random.permutation(jax.random.fold_in(own, 3), amount)
    giver, taker = mixed[0:amount // 2 * 2:2], mixed[1:amount // 2 * 2:2]
    margin = jnp.minimum(lengths[giver] - 1, bound - lengths[taker]) // 2
    margin = jnp.where((giver == ranking[0]) | (taker == ranking[0]) | (lengths[taker] == 0), 0, jnp.maximum(margin, 0))
    passed = jax.random.randint(jax.random.fold_in(own, 4), (amount // 2,), 0, 1 << 20) % (margin + 1)
    lengths = lengths.at[giver].add(-passed).at[taker].add(passed)
    labels = jnp.searchsorted(jnp.cumsum(lengths), jnp.arange(rows * top), side="right").astype(jnp.int32)
    listing = labels.reshape(top, rows).T
    listing = listing[jax.random.permutation(jax.random.fold_in(own, 1), rows)]
    offset_by = jax.random.randint(jax.random.fold_in(own, 2), (rows, 1), 0, top)
    return jnp.take_along_axis(listing, (jnp.arange(top)[None, :] + offset_by) % top, axis=1)


def portions_of(count, total, reach, skew, full):
    loads = [(1 << 20) // math.isqrt(grade ** skew) + 1 for grade in range(1, count + 1)]
    largest = reach if full else min(reach, max(-(-total // count), total * loads[0] // sum(loads)))
    least = 1 if total - largest >= count - 1 else 0
    given, rest = [largest] + [least] * (count - 1), total - largest - least * (count - 1)
    while rest > 0:
        free = [i for i in range(1, count) if given[i] < largest] or [i for i in range(1, count) if given[i] < reach]
        whole, remaining = sum([loads[i] for i in free]), rest
        for i in free:
            extra = min(reach - given[i], max(1, remaining * loads[i] // whole), rest)
            given[i] = given[i] + extra
            rest = rest - extra
    return np.array(given)


def normal_values(rng, shape, scale, reach, cuts=(), kind=jnp.bfloat16):
    level = shard_levels(rng, shape, cuts, -0.22, 0.18) if cuts else 1.0
    array = jax.random.normal(rng, shape, jnp.float32) * scale * level
    return jnp.minimum(jnp.maximum(array, -reach), reach).astype(kind)


def setup_inputs(seed: int = 0) -> dict:
    splits = jax.random.split(jax.random.key(seed), 9)
    tokens = normal_values(splits[0], (TOKENS, D), 1.0, 6.0, ((0, 32),))
    gate_weight = normal_values(splits[1], (EXPERTS, D, HID), RANK ** -0.5, 0.25, ((0, 16), (2, 2)))
    up_weight = normal_values(splits[2], (EXPERTS, D, HID), RANK ** -0.5, 0.25, ((0, 16), (2, 2)))
    down_weight = normal_values(splits[3], (EXPERTS, HID, D), HID ** -0.5, 0.1875, ((0, 16), (1, 2)))
    sketch = normal_values(splits[4], (EXPERTS, 2, HID, RANK), 1.0, 6.0, ((0, 16), (2, 2)))
    clusters = jnp.searchsorted(jnp.cumsum(uneven(splits[5], CLUSTERS, EXPERTS, MOST, 1)), jnp.arange(EXPERTS), side="right").astype(jnp.int32)
    routes_keys = jax.random.split(jax.random.fold_in(splits[6], 1), TOKENS // TOK_DEV)
    routes_turns = jax.random.permutation(jax.random.fold_in(splits[6], 3), TOKENS // TOK_DEV)
    routes = jax.vmap(lambda own, number: routed_block(jax.random.fold_in(splits[6], 2), own, number, TOK_DEV, EXPERTS, TOP, CAP, 2))(routes_keys, routes_turns).reshape((TOKENS, TOP))
    route_weights = jnp.clip(0.05 + 0.25 * jax.random.uniform(splits[7], (TOKENS, TOP), jnp.float32) ** shard_levels(splits[7], (TOKENS, TOP), ((0, 32),), -0.2, 0.2), 0.05, 0.3)
    return dict(tokens=tokens, gate_weight=gate_weight, up_weight=up_weight, down_weight=down_weight, sketch=sketch, clusters=clusters, routes=routes, route_weights=route_weights)


HIGHEST = lax.Precision.HIGHEST

def reference(tokens, gate_weight, up_weight, down_weight, sketch, clusters, routes, route_weights):
    experts = gate_weight.shape[0]
    indices = jnp.arange(experts, dtype=jnp.int32)

    def sketch_one(index):
        return jnp.dot(gate_weight[index].astype(jnp.float32), sketch[index, 0].astype(jnp.float32), preferred_element_type=jnp.float32) + jnp.dot(up_weight[index].astype(jnp.float32), sketch[index, 1].astype(jnp.float32), preferred_element_type=jnp.float32)
    sketched = lax.map(sketch_one, indices)
    same = (clusters[:, None] == clusters[None, :]).astype(jnp.float32)

    def compress(index):
        summed = jnp.tensordot(same[index], sketched, axes=1, precision=HIGHEST)
        gram = lax.dot_general(summed, summed, (((0,), (0,)), ((), ())), precision=HIGHEST)
        factor = jnp.linalg.cholesky(gram)
        basis = jax.scipy.linalg.solve_triangular(factor, summed.T, lower=True).T.astype(jnp.bfloat16)
        blocks = basis.reshape(N_TENSOR, -1, RANK).astype(jnp.float32)
        gate_blocks = gate_weight[index].reshape(N_TENSOR, -1, HID).astype(jnp.float32)
        up_blocks = up_weight[index].reshape(N_TENSOR, -1, HID).astype(jnp.float32)
        gate_parts = jnp.einsum('tdr,tdh->trh', blocks, gate_blocks, precision=HIGHEST).astype(jnp.bfloat16)
        up_parts = jnp.einsum('tdr,tdh->trh', blocks, up_blocks, precision=HIGHEST).astype(jnp.bfloat16)
        gate_parts, up_parts = lax.optimization_barrier((gate_parts, up_parts))
        gate_sum = jnp.sum(gate_parts.astype(jnp.float32), axis=0)
        up_sum = jnp.sum(up_parts.astype(jnp.float32), axis=0)
        return (basis, jnp.stack([gate_sum, up_sum]).astype(jnp.bfloat16))
    bases, coefficients = lax.map(compress, indices)
    targets = routes.reshape(-1)
    total_rows = targets.shape[0]
    top_count = routes.shape[1]
    token_count = tokens.shape[0]
    per_expert = N_EXPERT * N_DP * CAP
    onehot = (targets[:, None] == indices[None, :]).astype(jnp.int32)
    place = jnp.sum((jnp.cumsum(onehot, axis=0) - 1) * onehot, axis=1)
    slot_index = (targets * per_expert + place).astype(jnp.int32)
    owners = jnp.full((experts * per_expert,), token_count, jnp.int32)
    owners = owners.at[slot_index].set(jnp.arange(total_rows, dtype=jnp.int32) // top_count)
    owners = owners.reshape(experts, per_expert)
    padded = jnp.concatenate([tokens, jnp.zeros((1, tokens.shape[1]), jnp.bfloat16)], axis=0)

    def evaluate(index):
        gathered = padded[owners[index]]
        projected = jnp.dot(gathered.astype(jnp.float32), bases[index].astype(jnp.float32), preferred_element_type=jnp.float32).astype(jnp.bfloat16)
        gate_part = jnp.dot(projected.astype(jnp.float32), coefficients[index, 0].astype(jnp.float32), preferred_element_type=jnp.float32)
        up_part = jnp.dot(projected.astype(jnp.float32), coefficients[index, 1].astype(jnp.float32), preferred_element_type=jnp.float32)
        hidden = (jax.nn.silu(gate_part) * up_part).astype(jnp.bfloat16)
        return jnp.dot(hidden.astype(jnp.float32), down_weight[index].astype(jnp.float32), preferred_element_type=jnp.float32).astype(jnp.bfloat16)
    answers = lax.map(evaluate, indices).reshape(experts * per_expert, -1)
    slots = slot_index.reshape(token_count, top_count)
    mixed = jnp.zeros((token_count, tokens.shape[1]), jnp.float32)
    for column in range(top_count):
        mixed = mixed + answers[slots[:, column]].astype(jnp.float32) * route_weights[:, column][:, None]
    return mixed.astype(jnp.bfloat16)
```

```python
import jax
import jax.numpy as jnp
from jax import lax
from jax.sharding import PartitionSpec as P

MOST = 4


HIGHEST = lax.Precision.HIGHEST


def swap_in_group(value, mask):
    count = lax.axis_size("expert")
    return lax.ppermute(value, "expert", [(source, source ^ mask) for source in range(count)])


def shift_groups(value, steps):
    count = lax.axis_size("expert")
    moves = [(s, s + steps) for s in range(count) if 0 <= s + steps < count]
    return lax.ppermute(value, "expert", moves)


def cluster_rows(own, clusters):
    experts = lax.axis_size("expert")
    position = lax.axis_index("expert")
    place = position % MOST
    first = position - place
    got = [lax.dynamic_index_in_dim(own, place, 0, keepdims=False)]
    for mask in range(1, MOST):
        block = lax.dynamic_index_in_dim(own, place ^ mask, 0, keepdims=False)
        got.append(swap_in_group(block, mask))
    wide = [value.astype(jnp.float32) for value in got]
    names = [clusters[first + (place ^ mask)] for mask in range(MOST)]
    head_name, tail_name = clusters[first], clusters[first + MOST - 1]

    def chosen(name):
        return sum(jnp.where(names[k] == name, wide[k], 0.0) for k in range(MOST))

    from_below = shift_groups(chosen(tail_name).astype(jnp.bfloat16), MOST).astype(jnp.float32)
    from_above = shift_groups(chosen(head_name).astype(jnp.bfloat16), -MOST).astype(jnp.float32)
    below_name = jnp.where(first > 0, clusters[jnp.maximum(first - 1, 0)], -1)
    above_name = jnp.where(
        first + MOST < experts, clusters[jnp.minimum(first + MOST, experts - 1)], -1
    )
    back = []
    for mask in range(MOST):
        total = chosen(names[mask])
        total = total + jnp.where(names[mask] == below_name, from_below, 0.0)
        total = total + jnp.where(names[mask] == above_name, from_above, 0.0)
        total = total.astype(jnp.bfloat16)
        back.append(total if mask == 0 else swap_in_group(total, mask))
    stacked = jnp.stack(back)
    order = jnp.arange(MOST, dtype=jnp.int32) ^ place
    return stacked[order]


def on_device(tokens, gate_weight, up_weight, down_weight, sketch, clusters, routes, route_weights):
    experts = lax.axis_size("expert")
    position = lax.axis_index("expert")
    half = lax.axis_index("dp")
    dps = lax.axis_size("dp")
    gate_rows = gate_weight[0]
    up_rows = up_weight[0]
    depth, rank = gate_rows.shape[0], sketch.shape[-1]
    gathered = lax.all_gather(tokens, "expert", axis=0, tiled=True)
    down_rows = lax.all_gather(down_weight[0], "dp", axis=0, tiled=True)
    names = jnp.arange(experts, dtype=jnp.int32)
    shares = jnp.sum(
        jnp.where(routes[:, :, None] == names, route_weights[:, :, None], 0.0), axis=1
    )
    all_shares = lax.all_gather(shares, "expert", axis=0, tiled=True)
    share = lax.dynamic_slice_in_dim(all_shares, position, 1, axis=1)

    sketched = jnp.dot(gate_rows, sketch[0, 0], preferred_element_type=jnp.float32) + jnp.dot(
        up_rows, sketch[0, 1], preferred_element_type=jnp.float32
    )
    own_sketch = lax.psum_scatter(
        sketched.astype(jnp.bfloat16), "dp", scatter_dimension=0, tiled=True
    )
    blocks = own_sketch.reshape(MOST, depth // dps // MOST, rank)
    summed_half = cluster_rows(blocks, clusters).reshape(depth // dps, rank)
    summed = lax.all_gather(summed_half, "dp", axis=0, tiled=True)

    def crossed(right):
        return lax.dot_general(
            summed, right, (((0,), (0,)), ((), ())), preferred_element_type=jnp.float32
        )

    gram = lax.psum(crossed(summed), "tensor")
    raw = lax.psum(jnp.stack([crossed(gate_rows), crossed(up_rows)]), "tensor")
    raw_projected = lax.psum(
        jnp.dot(gathered, summed, preferred_element_type=jnp.float32), "tensor"
    )
    factor = jnp.linalg.cholesky(gram)
    inverse = jax.scipy.linalg.solve_triangular(
        factor, jnp.eye(rank, dtype=jnp.float32), lower=True
    )
    coeff_half = jnp.einsum("rs,gsh->grh", inverse, raw, precision=HIGHEST).astype(jnp.bfloat16)
    coefficients = lax.all_gather(coeff_half, "dp", axis=2, tiled=True)
    projected = lax.dot_general(
        raw_projected, inverse, (((1,), (1,)), ((), ())), precision=HIGHEST
    ).astype(jnp.bfloat16)
    gate_part = jnp.dot(projected, coefficients[0], preferred_element_type=jnp.float32)
    up_part = jnp.dot(projected, coefficients[1], preferred_element_type=jnp.float32)
    hidden = (jax.nn.silu(gate_part) * up_part).astype(jnp.bfloat16)
    answers = jnp.dot(hidden, down_rows, preferred_element_type=jnp.float32)
    weighted = (answers * share).astype(jnp.bfloat16)
    return lax.psum_scatter(weighted, "expert", scatter_dimension=0, tiled=True)


def solution(mesh):
    return jax.shard_map(
        on_device,
        mesh=mesh,
        in_specs=(
            P(("expert", "dp"), "tensor"),
            P("expert", "tensor", "dp"),
            P("expert", "tensor", "dp"),
            P("expert", "dp", "tensor"),
            P("expert", None, "dp", None),
            P(),
            P(("expert", "dp"), None),
            P(("expert", "dp"), None),
        ),
        out_specs=P(("expert", "dp"), "tensor"),
        check_vma=False,
    )
```

```python
import jax
import jax.numpy as jnp
from jax import lax
from jax.sharding import PartitionSpec as P

MOST = 4
CLUSTER_CHUNKS = 2
OUT_CHUNKS = 4

HIGHEST = lax.Precision.HIGHEST
HIGH = lax.Precision.HIGH


def swap_expert(value, mask):
    count = lax.axis_size("expert")
    return lax.ppermute(value, "expert", [(source, source ^ mask) for source in range(count)])


def swap_dp(value):
    count = lax.axis_size("dp")
    return lax.ppermute(value, "dp", [(source, count - 1 - source) for source in range(count)])


def shift_groups(value, steps):
    count = lax.axis_size("expert")
    moves = [(s, s + steps) for s in range(count) if 0 <= s + steps < count]
    return lax.ppermute(value, "expert", moves)


def cluster_rows(own, clusters):
    experts = lax.axis_size("expert")
    position = lax.axis_index("expert")
    place = position % MOST
    first = position - place
    wide = [own[0]]
    for mask in range(1, MOST):
        wide.append(swap_expert(own[mask], mask))
    wide = [value.astype(jnp.float32) for value in wide]
    names = [clusters[first + (place ^ mask)] for mask in range(MOST)]
    head_name, tail_name = clusters[first], clusters[first + MOST - 1]

    def chosen(name):
        return sum(jnp.where(names[k] == name, wide[k], 0.0) for k in range(MOST))

    from_below = shift_groups(chosen(tail_name).astype(jnp.bfloat16), MOST).astype(jnp.float32)
    from_above = shift_groups(chosen(head_name).astype(jnp.bfloat16), -MOST).astype(jnp.float32)
    below_name = jnp.where(first > 0, clusters[jnp.maximum(first - 1, 0)], -1)
    above_name = jnp.where(
        first + MOST < experts, clusters[jnp.minimum(first + MOST, experts - 1)], -1
    )
    totals = []
    for mask in range(MOST):
        total = chosen(names[mask])
        total = total + jnp.where(names[mask] == below_name, from_below, 0.0)
        total = total + jnp.where(names[mask] == above_name, from_above, 0.0)
        totals.append(total.astype(jnp.bfloat16))
    return totals


def relative(array, axis, size, index):
    return [
        lax.dynamic_index_in_dim(array, index ^ step, axis, keepdims=False) for step in range(size)
    ]


def on_device(tokens, gate_weight, up_weight, down_weight, sketch, clusters, routes, route_weights):
    experts = lax.axis_size("expert")
    position = lax.axis_index("expert")
    place = position % MOST
    groups = experts // MOST
    half = lax.axis_index("dp")
    dps = lax.axis_size("dp")
    gate_rows = gate_weight[0]
    up_rows = up_weight[0]
    depth, rank = gate_rows.shape[0], sketch.shape[-1]
    rows = depth // dps // MOST
    toks = tokens.shape[0]

    names = jnp.arange(experts, dtype=jnp.int32)
    shares = jnp.sum(
        jnp.where(routes[:, :, None] == names, route_weights[:, :, None], 0.0), axis=1
    )
    all_shares = lax.all_gather(shares, "expert", axis=0, tiled=False)
    share = lax.dynamic_index_in_dim(all_shares, position, 2, keepdims=False)
    share = share[names ^ position]

    down_rows = lax.all_gather(down_weight[0], "dp", axis=0, tiled=True)

    halves = jnp.stack(relative(tokens.reshape(toks, dps, MOST, rows), 1, dps, half), axis=1)
    token_blocks = relative(halves, 2, MOST, place)
    plane = [token_blocks[0]]
    for mask in range(1, MOST):
        plane.append(swap_expert(token_blocks[mask], mask))
    plane = jnp.stack(plane)
    spread = [plane]
    for step in range(1, groups):
        spread.append(swap_expert(plane, step * MOST))
    gathered = jnp.stack(spread).reshape(experts * toks, dps * rows)

    sketched = jnp.dot(gate_rows, sketch[0, 0], preferred_element_type=jnp.float32) + jnp.dot(
        up_rows, sketch[0, 1], preferred_element_type=jnp.float32
    )
    sketched = sketched.reshape(dps, MOST, rows, rank)
    own_half, other_half = relative(sketched, 0, dps, half)
    own_half = (own_half + swap_dp(other_half.astype(jnp.bfloat16)).astype(jnp.float32)).astype(
        jnp.bfloat16
    )
    own_blocks = relative(own_half, 0, MOST, place)
    chunk = rows // CLUSTER_CHUNKS
    pieces = [
        cluster_rows([block[c * chunk : (c + 1) * chunk] for block in own_blocks], clusters)
        for c in range(CLUSTER_CHUNKS)
    ]
    wide_pieces, own_pieces = [], []
    for piece in pieces:
        stacked = jnp.stack(piece)
        wide_pieces.append((stacked, swap_dp(stacked)))
        back = jnp.stack(
            [piece[0]] + [swap_expert(piece[mask], mask) for mask in range(1, MOST)]
        )
        own_pieces.append(jnp.stack([back, swap_dp(back)]))
    summed = jnp.concatenate(own_pieces, axis=2)
    group_sums = jnp.concatenate(
        [jnp.stack([own, other], axis=1) for own, other in wide_pieces], axis=2
    ).reshape(MOST, dps * rows, rank)

    parts = [
        jnp.dot(gathered, group_sums[k], preferred_element_type=jnp.float32) for k in range(MOST)
    ]
    raw_projected = parts[0].reshape(groups, MOST, toks, rank)
    for mask in range(1, MOST):
        arrived = swap_expert(parts[mask].astype(jnp.bfloat16), mask)
        arrived = arrived.reshape(groups, MOST, toks, rank).astype(jnp.float32)
        raw_projected = raw_projected + jnp.stack(
            [arrived[:, k ^ mask] for k in range(MOST)], axis=1
        )
    raw_projected = lax.psum(raw_projected.reshape(experts * toks, rank), "tensor")

    summed = jnp.stack(
        relative(jnp.stack(relative(summed, 1, MOST, place), axis=1), 0, dps, half)
    ).reshape(depth, rank)

    def crossed(right):
        return lax.dot_general(
            summed, right, (((0,), (0,)), ((), ())), preferred_element_type=jnp.float32
        )

    gram = lax.psum(crossed(summed), "tensor")
    raw = lax.psum(jnp.stack([crossed(gate_rows), crossed(up_rows)]), "tensor")
    factor = jnp.linalg.cholesky(gram)
    inverse = jax.scipy.linalg.solve_triangular(
        factor, jnp.eye(rank, dtype=jnp.float32), lower=True
    )
    coeff_half = jnp.einsum("rs,gsh->grh", inverse, raw, precision=HIGH).astype(jnp.bfloat16)
    both = jnp.stack([coeff_half, swap_dp(coeff_half)])
    both = relative(both, 0, dps, half)
    coefficients = jnp.concatenate(both, axis=2)
    projected = lax.dot_general(
        raw_projected, inverse, (((1,), (1,)), ((), ())), precision=HIGH
    ).astype(jnp.bfloat16)
    gate_part = jnp.dot(projected, coefficients[0], preferred_element_type=jnp.float32)
    up_part = jnp.dot(projected, coefficients[1], preferred_element_type=jnp.float32)
    hidden = (jax.nn.silu(gate_part) * up_part).astype(jnp.bfloat16)

    width = hidden.shape[1]
    hidden = hidden.reshape(groups, 2, 2, toks, width)
    share = share.reshape(groups, 2, 2, toks)
    chunks = OUT_CHUNKS if depth % (OUT_CHUNKS * 128) == 0 else 1
    cols = depth // chunks
    by_axis = []
    for axis in (2, 1):
        sides = []
        for side in (0, 1):
            picked = lax.index_in_dim(hidden, side, axis, keepdims=False).reshape(-1, width)
            weight = lax.index_in_dim(share, side, axis, keepdims=False).reshape(-1, 1)
            sides.append((picked, weight))
        by_axis.append(sides)

    def answered(side, c):
        picked, weight = side
        value = jnp.dot(
            picked, down_rows[:, c * cols : (c + 1) * cols], preferred_element_type=jnp.float32
        )
        return value * weight

    sent = []
    for c in range(chunks):
        order = c % 2
        outgoing = answered(by_axis[order][1], c).astype(jnp.bfloat16)
        sent.append(swap_expert(outgoing, 1 << order))
    outs = []
    for c in range(chunks):
        order = c % 2
        value = answered(by_axis[order][0], c) + sent[c].astype(jnp.float32)
        value = value.astype(jnp.bfloat16).reshape(groups, 2, toks, cols)
        kept = value[:, 0].astype(jnp.float32) + swap_expert(value[:, 1], 2 >> order).astype(
            jnp.float32
        )
        kept = kept.astype(jnp.bfloat16)
        total = kept[0].astype(jnp.float32)
        for step in range(1, groups):
            total = total + swap_expert(kept[step], step * MOST).astype(jnp.float32)
        outs.append(total.astype(jnp.bfloat16))
    return jnp.concatenate(outs, axis=1)


def solution(mesh):
    return jax.shard_map(
        on_device,
        mesh=mesh,
        in_specs=(
            P(("expert", "dp"), "tensor"),
            P("expert", "tensor", "dp"),
            P("expert", "tensor", "dp"),
            P("expert", "dp", "tensor"),
            P("expert", None, "dp", None),
            P(),
            P(("expert", "dp"), None),
            P(("expert", "dp"), None),
        ),
        out_specs=P(("expert", "dp"), "tensor"),
        check_vma=False,
    )
```

```python
import functools

import jax
import jax.numpy as jnp
from jax import lax
from jax.experimental import pallas as pl
from jax.experimental.pallas import tpu as pltpu
from jax.sharding import PartitionSpec as P

MOST = 4
LANES = 128
VMEM_BYTES = 56 * 1024 * 1024

HIGHEST = lax.Precision.HIGHEST
F32 = jnp.float32
BF16 = jnp.bfloat16


def swap_expert(value, mask):
    count = lax.axis_size("expert")
    return lax.ppermute(value, "expert", [(source, source ^ mask) for source in range(count)])


def swap_dp(value):
    count = lax.axis_size("dp")
    return lax.ppermute(value, "dp", [(source, count - 1 - source) for source in range(count)])


def shift_groups(value, steps):
    count = lax.axis_size("expert")
    moves = [(s, s + steps) for s in range(count) if 0 <= s + steps < count]
    return lax.ppermute(value, "expert", moves)


def whole():
    return pl.BlockSpec(memory_space=pltpu.VMEM)


def scalars():
    return pl.BlockSpec(memory_space=pltpu.SMEM)


def params(**more):
    return pltpu.CompilerParams(vmem_limit_bytes=VMEM_BYTES, **more)


def cost(flops, moved):
    return pl.CostEstimate(flops=int(flops), bytes_accessed=int(moved), transcendentals=0)


def mul(a, b, dims=((1,), (0,))):
    return lax.dot_general(a, b, (dims, ((), ())), preferred_element_type=F32)


def exact(a, b, dims):
    return lax.dot_general(a, b, (dims, ((), ())), precision=HIGHEST, preferred_element_type=F32)


def parts_of(value):
    high = value.astype(BF16)
    return high, (value - high.astype(F32)).astype(BF16)


def mul3(a, b, dims):
    (a0, a1), (b0, b1) = parts_of(a), parts_of(b)
    return mul(a0, b0, dims) + (mul(a0, b1, dims) + mul(a1, b0, dims))


def token_kernel(groups, rows, meta, tokens, routes, weights, *pieces):
    place = lax.rem(meta[2 * MOST], MOST)
    toks = tokens.shape[0]
    lane = lax.broadcasted_iota(jnp.int32, (toks, LANES), 1)
    group = lax.rem(lane, groups)
    for k in range(MOST):
        expert = group * MOST + (place ^ k)
        share = jnp.zeros((toks, LANES), F32)
        for t in range(routes.shape[1]):
            share += jnp.where(routes[:, t : t + 1] == expert, weights[:, t : t + 1], 0.0)
        high, low = parts_of(share)
        pieces[k][:, :LANES] = jnp.where(
            lane < groups, high.astype(F32), low.astype(F32)
        ).astype(BF16)
        for d in range(2):
            start = pl.multiple_of(meta[d * MOST + k] * rows, LANES)
            pieces[k][:, LANES + d * rows : LANES + (d + 1) * rows] = tokens[:, pl.ds(start, rows)]


def token_pieces(meta, tokens, routes, weights, groups, rows, place):
    toks = tokens.shape[0]
    if rows % LANES == 0:
        return pl.pallas_call(
            functools.partial(token_kernel, groups, rows),
            out_shape=[jax.ShapeDtypeStruct((toks, LANES + 2 * rows), BF16)] * MOST,
            in_specs=[scalars(), whole(), whole(), whole()],
            out_specs=[whole()] * MOST,
            compiler_params=params(),
            name="token_pieces",
        )(meta, tokens, routes, weights)
    lane = jnp.arange(LANES, dtype=jnp.int32)
    pieces = []
    for k in range(MOST):
        expert = (lane % groups) * MOST + (place ^ k)
        share = jnp.sum(jnp.where(routes[:, :, None] == expert, weights[:, :, None], 0.0), axis=1)
        high, low = parts_of(share)
        columns = [
            lax.dynamic_slice_in_dim(tokens, meta[d * MOST + k] * rows, rows, axis=1)
            for d in range(2)
        ]
        pieces.append(jnp.concatenate([jnp.where(lane < groups, high, low)] + columns, axis=1))
    return pieces


def sketch_kernel(meta, gate, up, sketch, out):
    value = mul(gate[...], sketch[0]) + mul(up[...], sketch[1])
    out[0] = value.astype(out.dtype)


def sketch_half(meta, gate, up, sketch, side, dtype, rows):
    hid, rank = sketch.shape[1:]
    row_block = pl.BlockSpec((rows, hid), lambda k, meta: (meta[side * MOST + k], 0))
    return pl.pallas_call(
        sketch_kernel,
        grid_spec=pltpu.PrefetchScalarGridSpec(
            num_scalar_prefetch=1,
            grid=(MOST,),
            in_specs=[row_block, row_block, pl.BlockSpec((2, hid, rank), lambda k, meta: (0, 0, 0))],
            out_specs=pl.BlockSpec((1, rows, rank), lambda k, meta: (k, 0, 0)),
        ),
        out_shape=jax.ShapeDtypeStruct((MOST, rows, rank), dtype),
        compiler_params=params(),
        cost_estimate=cost(4 * MOST * rows * hid * rank, 4 * MOST * rows * hid),
        name="sketch_half",
    )(meta, gate, up, sketch)


def chosen(values, names, name):
    total = jnp.zeros(values[0].shape, F32)
    for value, own in zip(values, names):
        total += jnp.where(own == name, value, 0.0)
    return total


def ends_kernel(meta, *refs):
    values = [ref[...].astype(F32) for ref in refs[:MOST]]
    tail, head = refs[MOST:]
    position = meta[2 * MOST]
    place = lax.rem(position, MOST)
    first = position - place
    base = 2 * MOST + 1
    names = [meta[base + first + (place ^ k)] for k in range(MOST)]
    tail[...] = chosen(values, names, meta[base + first + MOST - 1]).astype(BF16)
    head[...] = chosen(values, names, meta[base + first]).astype(BF16)


def totals_kernel(experts, meta, *refs):
    values = [ref[...].astype(F32) for ref in refs[:MOST]]
    below, above = (ref[...].astype(F32) for ref in refs[MOST : MOST + 2])
    stacked, sends = refs[MOST + 2], refs[MOST + 3 :]
    position = meta[2 * MOST]
    place = lax.rem(position, MOST)
    first = position - place
    base = 2 * MOST + 1
    names = [meta[base + first + (place ^ k)] for k in range(MOST)]
    below_name = jnp.where(first > 0, meta[base + jnp.maximum(first - 1, 0)], -1)
    above_name = jnp.where(
        first + MOST < experts, meta[base + jnp.minimum(first + MOST, experts - 1)], -1
    )
    for k in range(MOST):
        total = chosen(values, names, names[k])
        total += jnp.where(names[k] == below_name, below, 0.0)
        total += jnp.where(names[k] == above_name, above, 0.0)
        total = total.astype(BF16)
        stacked[k] = total
        if k:
            sends[k - 1][...] = total


def stack_kernel(*refs):
    for k in range(MOST):
        refs[MOST][k] = refs[k][...]


def cluster_rows(meta, own):
    shape = own[0].shape
    experts = lax.axis_size("expert")
    got = [own[0]] + [swap_expert(own[k], k) for k in range(1, MOST)]
    piece = jax.ShapeDtypeStruct(shape, BF16)
    stacked = jax.ShapeDtypeStruct((MOST,) + shape, BF16)
    tail, head = pl.pallas_call(
        ends_kernel,
        out_shape=[piece, piece],
        in_specs=[scalars()] + [whole()] * MOST,
        out_specs=[whole()] * 2,
        compiler_params=params(),
        name="end_sums",
    )(meta, *got)
    below = shift_groups(tail, MOST)
    above = shift_groups(head, -MOST)
    sums, *sends = pl.pallas_call(
        functools.partial(totals_kernel, experts),
        out_shape=[stacked] + [piece] * (MOST - 1),
        in_specs=[scalars()] + [whole()] * (MOST + 2),
        out_specs=[whole()] * MOST,
        compiler_params=params(),
        name="cluster_sums",
    )(meta, *got, below, above)
    back = [sums[0]] + [swap_expert(sends[k - 1], k) for k in range(1, MOST)]
    mine = pl.pallas_call(
        stack_kernel,
        out_shape=stacked,
        in_specs=[whole()] * MOST,
        out_specs=whole(),
        compiler_params=params(),
        name="own_sums",
    )(*back)
    return sums, mine


def cross_kernel(started, meta, own, other, gate, up, *refs):
    if started:
        old_gram, old_raw, gram, raw, current = refs
    else:
        gram, raw, current = refs
    step = pl.program_id(0)

    @pl.when(step == 0)
    def _():
        gram[...] = old_gram[...] if started else jnp.zeros(gram.shape, F32)
        raw[...] = old_raw[...] if started else jnp.zeros(raw.shape, F32)

    @pl.when(step < MOST)
    def _():
        current[...] = own[0]

    @pl.when(step >= MOST)
    def _():
        current[...] = other[0]

    rows = current[...]
    turned = rows.T
    gram[...] += mul(turned, rows)
    raw[0] += mul(turned, gate[...])
    raw[1] += mul(turned, up[...])


def crossed(meta, own, other, gate, up, chunk, chunks, before):
    _, rows, rank = own.shape
    hid = gate.shape[1]
    row_block = pl.BlockSpec((rows, hid), lambda i, meta: (meta[i] * chunks + chunk, 0))
    gram_spec = pl.BlockSpec((rank, rank), lambda i, meta: (0, 0))
    raw_spec = pl.BlockSpec((2, rank, hid), lambda i, meta: (0, 0, 0))
    return pl.pallas_call(
        functools.partial(cross_kernel, bool(before)),
        grid_spec=pltpu.PrefetchScalarGridSpec(
            num_scalar_prefetch=1,
            grid=(2 * MOST,),
            in_specs=[
                pl.BlockSpec((1, rows, rank), lambda i, meta: (jnp.minimum(i, MOST - 1), 0, 0)),
                pl.BlockSpec((1, rows, rank), lambda i, meta: (jnp.maximum(i - MOST, 0), 0, 0)),
                row_block,
                row_block,
            ]
            + ([gram_spec, raw_spec] if before else []),
            out_specs=[gram_spec, raw_spec],
            scratch_shapes=[pltpu.VMEM((rows, rank), BF16)],
        ),
        out_shape=[
            jax.ShapeDtypeStruct((rank, rank), F32),
            jax.ShapeDtypeStruct((2, rank, hid), F32),
        ],
        compiler_params=params(),
        cost_estimate=cost(4 * MOST * rows * rank * (rank + 2 * hid), 8 * MOST * rows * rank * 3),
        name="crossed",
    )(meta, own, other, gate, up, *before)


def project_kernel(chunks, *refs):
    tokens, refs = refs[: -2 * chunks - 2], refs[-2 * chunks - 2 :]
    sums, out, basis = refs[: 2 * chunks], refs[-2], refs[-1]
    rows = sums[0].shape[1]
    for i, ref in enumerate(sums):
        basis[i * rows : (i + 1) * rows, :] = ref[0]
    toks = tokens[0].shape[0]
    for i, ref in enumerate(tokens):
        out[0, i * toks : (i + 1) * toks] = mul(ref[:, LANES:], basis[...]).astype(BF16)


def project(tokens, sums):
    rank = sums[0].shape[-1]
    toks, width = tokens[0].shape
    depth = width - LANES
    total = len(tokens) * toks
    return pl.pallas_call(
        functools.partial(project_kernel, len(sums) // 2),
        grid=(MOST,),
        in_specs=[pl.BlockSpec((toks, width), lambda k: (0, 0))] * len(tokens)
        + [pl.BlockSpec((1,) + value.shape[1:], lambda k: (k, 0, 0)) for value in sums],
        out_specs=pl.BlockSpec((1, total, rank), lambda k: (k, 0, 0)),
        out_shape=jax.ShapeDtypeStruct((MOST, total, rank), BF16),
        scratch_shapes=[pltpu.VMEM((depth, rank), BF16)],
        compiler_params=params(),
        cost_estimate=cost(2 * MOST * total * depth * rank, 4 * MOST * total * rank),
        name="project",
    )(*tokens, *sums)


def factor_kernel(tile, gram_ref, raw_ref, inverse_ref, coeff_ref, work_ref):
    rank = gram_ref.shape[0]
    steps = rank // tile
    work_ref[...] = gram_ref[...]
    row_of = lax.broadcasted_iota(jnp.int32, (tile, tile), 0)
    col_of = lax.broadcasted_iota(jnp.int32, (tile, tile), 1)
    lane = lax.broadcasted_iota(jnp.int32, (8, tile), 1)
    sub = lax.broadcasted_iota(jnp.int32, (8, tile), 0)
    lane_row = lane[:1]

    def step(index, carry):
        base = pl.multiple_of(index * tile, tile)
        here = pl.ds(base, tile)
        strips = [
            work_ref[pl.ds(pl.multiple_of(base + 8 * s, 8), 8), here] for s in range(tile // 8)
        ]
        for j in range(tile):
            first, inner = divmod(j, 8)
            row = strips[first][inner : inner + 1, :]
            pivot = 1.0 / row[:, j : j + 1]
            scaled = jnp.where(lane_row == j, 1.0, row) * pivot
            for s in range(first, tile // 8):
                strip = strips[s]
                column = strip[:, j : j + 1]
                new = jnp.where(lane == j, 0.0, strip) - column * scaled
                strips[s] = jnp.where(sub > inner, new, strip) if s == first else new
        block = jnp.concatenate(strips, axis=0)
        pivots = jnp.sum(jnp.where(row_of == col_of, block, 0.0), axis=1, keepdims=True)
        unit = jnp.where(row_of == col_of, 1.0, 0.0)
        own = jnp.where(col_of < row_of, block, unit) / jnp.sqrt(pivots)
        work_ref[here, here] = unit
        right = exact(own, work_ref[here, :], ((1,), (0,)))
        columns = lax.broadcasted_iota(jnp.int32, (tile, rank), 1)
        inverse_ref[here, :] = jnp.where(columns < base + tile, right, 0.0)
        for s in range(steps - 1):

            @pl.when(index == s)
            def _():
                below = slice((s + 1) * tile, rank)
                mine = slice(s * tile, (s + 1) * tile)
                left = exact(work_ref[below, mine], own, ((1,), (1,)))
                work_ref[below, mine] = jnp.zeros((rank - (s + 1) * tile, tile), F32)
                work_ref[below, :] = work_ref[below, :] - exact(left, right, ((1,), (0,)))

        return carry

    lax.fori_loop(0, steps, step, 0)
    inverse = inverse_ref[...]
    for side in range(2):
        coeff_ref[side] = mul3(inverse, raw_ref[side], ((1,), (0,))).astype(BF16)


def factored(gram, raw):
    rank = gram.shape[0]
    return pl.pallas_call(
        functools.partial(factor_kernel, min(LANES, rank)),
        out_shape=[
            jax.ShapeDtypeStruct((rank, rank), F32),
            jax.ShapeDtypeStruct(raw.shape, BF16),
        ],
        in_specs=[whole()] * 2,
        out_specs=[whole()] * 2,
        scratch_shapes=[pltpu.VMEM((rank, rank), F32)],
        compiler_params=params(),
        cost_estimate=cost(4e10, 8 * rank * rank),
        name="factored",
    )(gram, raw)


def hidden_kernel(toks, groups, meta, inverse, mine, others, tokens, *refs):
    arrived, outs = refs[:MOST], refs[MOST:]
    group = meta[2 * MOST] // MOST
    lane = lax.broadcasted_iota(jnp.int32, tokens.shape, 1)
    picked = (lane == group) | (lane == group + groups)
    share = jnp.sum(jnp.where(picked, tokens[...].astype(F32), 0.0), axis=1, keepdims=True)
    raw = []
    for k in range(MOST):
        total = jnp.zeros((toks, inverse.shape[0]), F32)
        for mask in range(MOST):
            source = (k ^ mask) * toks
            total += arrived[mask][source : source + toks, :].astype(F32)
        raw.append(total)
    projected = mul3(jnp.concatenate(raw, axis=0), inverse[...], ((1,), (1,))).astype(BF16)
    hid = mine.shape[2]
    for d, side in enumerate((mine, others)):
        gate = mul(projected, side[0])
        hidden = gate / (1.0 + jnp.exp(-gate)) * mul(projected, side[1]) * share
        hidden = hidden.astype(BF16)
        block = pl.ds(pl.multiple_of(meta[d * MOST] // MOST * hid, LANES), hid)
        for k in range(MOST):
            x, y = k % 2, k // 2
            rows = hidden[k * toks : (k + 1) * toks]
            outs[x][0, y * toks : (y + 1) * toks, block] = rows
            outs[2 + y][0, x * toks : (x + 1) * toks, block] = rows


def hidden_rows(meta, inverse, coeff, other_coeff, tokens, arrived, toks):
    rank, hid = coeff.shape[1:]
    groups = tokens.shape[0] // (MOST * toks)
    block = MOST * toks
    out = jax.ShapeDtypeStruct((groups, block // 2, 2 * hid), BF16)
    coeff_spec = pl.BlockSpec((2, rank, hid), lambda g: (0, 0, 0))
    return pl.pallas_call(
        functools.partial(hidden_kernel, toks, groups),
        grid=(groups,),
        in_specs=[
            scalars(),
            pl.BlockSpec((rank, rank), lambda g: (0, 0)),
            coeff_spec,
            coeff_spec,
            pl.BlockSpec((block, LANES), lambda g: (g, 0)),
        ]
        + [pl.BlockSpec((block, rank), lambda g: (g, 0))] * MOST,
        out_specs=[pl.BlockSpec((1, block // 2, 2 * hid), lambda g: (g, 0, 0))] * 4,
        out_shape=[out] * 4,
        compiler_params=params(),
        cost_estimate=cost(groups * block * rank * (6 * rank + 8 * hid), 16 * groups * block * hid),
        name="hidden_rows",
    )(meta, inverse, coeff, other_coeff, tokens, *arrived)


def column_chunks(depth):
    units = depth // LANES
    if units % 2 or units < 6:
        return [(0, depth, 0)]
    left = units // 2
    sizes = [left * 12 // 28, left * 10 // 28]
    sizes.append(left - sum(sizes))
    chunks, start = [], 0
    for size in sizes:
        for order in range(2):
            chunks.append((start, size * LANES, order))
            start += size * LANES
    return chunks


def scattered_answers(sides, down, toks):
    depth = down.shape[1]
    experts = lax.axis_size("expert")
    chunks = column_chunks(depth)

    def answered(rows, start, width):
        return mul(rows.reshape(-1, rows.shape[-1]), down[:, start : start + width])

    first = [answered(sides[2 * order + 1], start, width).astype(BF16) for start, width, order in chunks]
    pairs = [list(range(i, min(i + 2, len(chunks)))) for i in range(0, len(chunks), 2)]
    outs = []
    held = None
    for pair in pairs:
        outgoing = [first[i] for i in pair]
        if held is not None:
            tied = lax.optimization_barrier(tuple(outgoing) + tuple(held))
            outgoing, held = list(tied[: len(pair)]), list(tied[len(pair) :])
            finish(held_kept, held, outs, toks, experts)
        came = [swap_expert(value, 1 << chunks[i][2]) for value, i in zip(outgoing, pair)]
        kept, sends = [], []
        for value, i in zip(came, pair):
            start, width, order = chunks[i]
            total = answered(sides[2 * order], start, width) + value.astype(F32)
            total = total.astype(BF16).reshape(-1, 2, toks, width)
            kept.append((total[:, 0], 2 >> order))
            sends.append(total[:, 1])
        held, held_kept = sends, kept
    finish(held_kept, held, outs, toks, experts)
    return jnp.concatenate(outs, axis=1)


def finish(kept, sends, outs, toks, experts):
    for (mine, mask), outgoing in zip(kept, sends):
        value = mine.astype(F32) + swap_expert(outgoing, mask).astype(F32)
        bit = MOST
        while bit < experts:
            value = value.astype(BF16).reshape(-1, 2, toks, value.shape[-1])
            value = value[:, 0].astype(F32) + swap_expert(value[:, 1], bit).astype(F32)
            bit *= 2
        outs.append(value[0].astype(BF16))


def on_device(tokens, gate_weight, up_weight, down_weight, sketch, clusters, routes, route_weights):
    experts = lax.axis_size("expert")
    position = lax.axis_index("expert").astype(jnp.int32)
    place = position % MOST
    groups = experts // MOST
    half = lax.axis_index("dp").astype(jnp.int32)
    gate_rows = gate_weight[0]
    up_rows = up_weight[0]
    depth, rank = gate_rows.shape[0], sketch.shape[-1]
    rows = depth // 2 // MOST
    toks = tokens.shape[0]
    steps = jnp.arange(2 * MOST, dtype=jnp.int32)
    order = ((steps // MOST) ^ half) * MOST + ((steps % MOST) ^ place)
    meta = jnp.concatenate([order, position[None], clusters])

    down_rows = lax.all_gather(down_weight[0], "dp", axis=0, tiled=True)

    sent_half = swap_dp(sketch_half(meta, gate_rows, up_rows, sketch[0], 1, BF16, rows))
    own_half = sketch_half(meta, gate_rows, up_rows, sketch[0], 0, F32, rows)
    pieces = token_pieces(meta, tokens, routes, route_weights, groups, rows, place)
    plane = [pieces[0]] + [swap_expert(pieces[k], k) for k in range(1, MOST)]
    plane = jnp.concatenate(plane, axis=0)
    spread = [plane] + [swap_expert(plane, step * MOST) for step in range(1, groups)]

    chunks = 2 if rows % 32 == 0 else 1
    chunk = rows // chunks
    group_sums, own_sums = [], []
    for c in range(chunks):
        span = slice(c * chunk, (c + 1) * chunk)
        own = [
            (own_half[k, span] + sent_half[k, span].astype(F32)).astype(BF16) for k in range(MOST)
        ]
        sums, mine = cluster_rows(meta, own)
        group_sums.append((sums, swap_dp(sums)))
        own_sums.append((mine, swap_dp(mine)))

    parts = project(spread, [sums[d] for d in range(2) for sums in group_sums])
    before = ()
    for c in range(chunks):
        before = crossed(meta, *own_sums[c], gate_rows, up_rows, c, chunks, before)
    gram, raw = before
    if lax.axis_size("tensor") > 1:
        gram, raw = lax.psum((gram, raw), "tensor")
        parts = lax.psum(parts.astype(F32), "tensor").astype(BF16)
    gram, raw, parts = lax.optimization_barrier((gram, raw, parts))
    arrived = [parts[0]] + [swap_expert(parts[k], k) for k in range(1, MOST)]
    inverse, coeff = factored(gram, raw)
    other_coeff = swap_dp(coeff)
    shares = jnp.concatenate([value[:, :LANES] for value in spread], axis=0)
    sides = hidden_rows(meta, inverse, coeff, other_coeff, shares, arrived, toks)
    return scattered_answers(sides, down_rows, toks)


def solution(mesh):
    return jax.shard_map(
        on_device,
        mesh=mesh,
        in_specs=(
            P(("expert", "dp"), "tensor"),
            P("expert", "tensor", "dp"),
            P("expert", "tensor", "dp"),
            P("expert", "dp", "tensor"),
            P("expert", None, "dp", None),
            P(),
            P(("expert", "dp"), None),
            P(("expert", "dp"), None),
        ),
        out_specs=P(("expert", "dp"), "tensor"),
        check_vma=False,
    )
```

```python
import functools

import jax
import jax.numpy as jnp
from jax import lax
from jax.experimental import pallas as pl
from jax.experimental.pallas import tpu as pltpu
from jax.sharding import PartitionSpec as P

MOST = 4
LANES = 128
VMEM_BYTES = 56 * 1024 * 1024

HIGHEST = lax.Precision.HIGHEST
F32 = jnp.float32
BF16 = jnp.bfloat16


def swap_expert(value, mask):
    count = lax.axis_size("expert")
    return lax.ppermute(value, "expert", [(source, source ^ mask) for source in range(count)])


def swap_dp(value):
    count = lax.axis_size("dp")
    return lax.ppermute(value, "dp", [(source, count - 1 - source) for source in range(count)])


def shift_groups(value, steps):
    count = lax.axis_size("expert")
    moves = [(s, s + steps) for s in range(count) if 0 <= s + steps < count]
    return lax.ppermute(value, "expert", moves)


def whole():
    return pl.BlockSpec(memory_space=pltpu.VMEM)


def scalars():
    return pl.BlockSpec(memory_space=pltpu.SMEM)


def params(**more):
    return pltpu.CompilerParams(vmem_limit_bytes=VMEM_BYTES, **more)


def cost(flops, moved):
    return pl.CostEstimate(flops=int(flops), bytes_accessed=int(moved), transcendentals=0)


def mul(a, b, dims=((1,), (0,))):
    return lax.dot_general(a, b, (dims, ((), ())), preferred_element_type=F32)


def exact(a, b, dims):
    return lax.dot_general(a, b, (dims, ((), ())), precision=HIGHEST, preferred_element_type=F32)


def parts_of(value):
    high = value.astype(BF16)
    return high, (value - high.astype(F32)).astype(BF16)


def mul3(a, b, dims):
    (a0, a1), (b0, b1) = parts_of(a), parts_of(b)
    return mul(a0, b0, dims) + (mul(a0, b1, dims) + mul(a1, b0, dims))


def token_kernel(groups, rows, meta, tokens, routes, weights, *pieces):
    place = lax.rem(meta[2 * MOST], MOST)
    toks = tokens.shape[0]
    lane = lax.broadcasted_iota(jnp.int32, (toks, LANES), 1)
    group = lax.rem(lane, groups)
    for k in range(MOST):
        expert = group * MOST + (place ^ k)
        share = jnp.zeros((toks, LANES), F32)
        for t in range(routes.shape[1]):
            share += jnp.where(routes[:, t : t + 1] == expert, weights[:, t : t + 1], 0.0)
        high, low = parts_of(share)
        pieces[k][:, :LANES] = jnp.where(
            lane < groups, high.astype(F32), low.astype(F32)
        ).astype(BF16)
        for d in range(2):
            start = pl.multiple_of(meta[d * MOST + k] * rows, LANES)
            pieces[k][:, LANES + d * rows : LANES + (d + 1) * rows] = tokens[:, pl.ds(start, rows)]


def token_pieces(meta, tokens, routes, weights, groups, rows, place):
    toks = tokens.shape[0]
    if rows % LANES == 0:
        return pl.pallas_call(
            functools.partial(token_kernel, groups, rows),
            out_shape=[jax.ShapeDtypeStruct((toks, LANES + 2 * rows), BF16)] * MOST,
            in_specs=[scalars(), whole(), whole(), whole()],
            out_specs=[whole()] * MOST,
            compiler_params=params(),
            name="token_pieces",
        )(meta, tokens, routes, weights)
    lane = jnp.arange(LANES, dtype=jnp.int32)
    pieces = []
    for k in range(MOST):
        expert = (lane % groups) * MOST + (place ^ k)
        share = jnp.sum(jnp.where(routes[:, :, None] == expert, weights[:, :, None], 0.0), axis=1)
        high, low = parts_of(share)
        columns = [
            lax.dynamic_slice_in_dim(tokens, meta[d * MOST + k] * rows, rows, axis=1)
            for d in range(2)
        ]
        pieces.append(jnp.concatenate([jnp.where(lane < groups, high, low)] + columns, axis=1))
    return pieces


def sketch_kernel(meta, gate, up, sketch, out):
    both = jnp.concatenate([gate[...], up[...]], axis=1)
    out[0] = mul(both, jnp.concatenate([sketch[0], sketch[1]], axis=0)).astype(BF16)


def sketch_half(meta, gate, up, sketch, side, rows):
    hid, rank = sketch.shape[1:]
    row_block = pl.BlockSpec((rows, hid), lambda k, meta: (meta[side * MOST + k], 0))
    return pl.pallas_call(
        sketch_kernel,
        grid_spec=pltpu.PrefetchScalarGridSpec(
            num_scalar_prefetch=1,
            grid=(MOST,),
            in_specs=[row_block, row_block, pl.BlockSpec((2, hid, rank), lambda k, meta: (0, 0, 0))],
            out_specs=pl.BlockSpec((1, rows, rank), lambda k, meta: (k, 0, 0)),
        ),
        out_shape=jax.ShapeDtypeStruct((MOST, rows, rank), BF16),
        compiler_params=params(),
        cost_estimate=cost(4 * MOST * rows * hid * rank, 4 * MOST * rows * hid),
        name="sketch_half",
    )(meta, gate, up, sketch)


def chosen(values, names, name):
    total = jnp.zeros(values[0].shape, F32)
    for value, own in zip(values, names):
        total += jnp.where(own == name, value, 0.0)
    return total


def ends_kernel(meta, *refs):
    values = [ref[...].astype(F32) for ref in refs[:MOST]]
    tail, head = refs[MOST:]
    position = meta[2 * MOST]
    place = lax.rem(position, MOST)
    first = position - place
    base = 2 * MOST + 1
    names = [meta[base + first + (place ^ k)] for k in range(MOST)]
    tail[...] = chosen(values, names, meta[base + first + MOST - 1]).astype(BF16)
    head[...] = chosen(values, names, meta[base + first]).astype(BF16)


def totals_kernel(experts, meta, *refs):
    values = [ref[...].astype(F32) for ref in refs[:MOST]]
    below, above = (ref[...].astype(F32) for ref in refs[MOST : MOST + 2])
    stacked, sends = refs[MOST + 2], refs[MOST + 3 :]
    position = meta[2 * MOST]
    place = lax.rem(position, MOST)
    first = position - place
    base = 2 * MOST + 1
    names = [meta[base + first + (place ^ k)] for k in range(MOST)]
    below_name = jnp.where(first > 0, meta[base + jnp.maximum(first - 1, 0)], -1)
    above_name = jnp.where(
        first + MOST < experts, meta[base + jnp.minimum(first + MOST, experts - 1)], -1
    )
    for k in range(MOST):
        total = chosen(values, names, names[k])
        total += jnp.where(names[k] == below_name, below, 0.0)
        total += jnp.where(names[k] == above_name, above, 0.0)
        total = total.astype(BF16)
        stacked[k] = total
        if k:
            sends[k - 1][...] = total


def stack_kernel(*refs):
    for k in range(MOST):
        refs[MOST][k] = refs[k][...]


def cluster_rows(meta, got, riders):
    shape = got[0].shape
    experts = lax.axis_size("expert")
    piece = jax.ShapeDtypeStruct(shape, BF16)
    stacked = jax.ShapeDtypeStruct((MOST,) + shape, BF16)
    tail, head = pl.pallas_call(
        ends_kernel,
        out_shape=[piece, piece],
        in_specs=[scalars()] + [whole()] * MOST,
        out_specs=[whole()] * 2,
        compiler_params=params(),
        name="end_sums",
    )(meta, *got)
    below = shift_groups(tail, MOST)
    above = shift_groups(head, -MOST)
    below, above, riders = lax.optimization_barrier((below, above, riders))
    sums, *sends = pl.pallas_call(
        functools.partial(totals_kernel, experts),
        out_shape=[stacked] + [piece] * (MOST - 1),
        in_specs=[scalars()] + [whole()] * (MOST + 2),
        out_specs=[whole()] * MOST,
        compiler_params=params(),
        name="cluster_sums",
    )(meta, *got, below, above)
    back = [sums[0]] + [swap_expert(sends[k - 1], k) for k in range(1, MOST)]
    mine = pl.pallas_call(
        stack_kernel,
        out_shape=stacked,
        in_specs=[whole()] * MOST,
        out_specs=whole(),
        compiler_params=params(),
        name="own_sums",
    )(*back)
    return sums, mine, riders


def cross_kernel(started, meta, own, other, gate, gate_other, up, up_other, *refs):
    if started:
        old_gram, old_raw, gram, raw = refs
    else:
        gram, raw = refs
    step = pl.program_id(0)

    @pl.when(step == 0)
    def _():
        gram[...] = old_gram[...] if started else jnp.zeros(gram.shape, F32)
        raw[...] = old_raw[...] if started else jnp.zeros(raw.shape, F32)

    rows = jnp.concatenate([own[0], other[0]], axis=0)
    turned = rows.T
    gram[...] += mul(turned, rows)
    raw[0] += mul(turned, jnp.concatenate([gate[...], gate_other[...]], axis=0))
    raw[1] += mul(turned, jnp.concatenate([up[...], up_other[...]], axis=0))


def crossed(meta, own, other, gate, up, chunk, chunks, before):
    _, rows, rank = own.shape
    hid = gate.shape[1]
    sum_block = pl.BlockSpec((1, rows, rank), lambda i, meta: (i, 0, 0))
    row_block = pl.BlockSpec((rows, hid), lambda i, meta: (meta[i] * chunks + chunk, 0))
    other_block = pl.BlockSpec((rows, hid), lambda i, meta: (meta[MOST + i] * chunks + chunk, 0))
    gram_spec = pl.BlockSpec((rank, rank), lambda i, meta: (0, 0))
    raw_spec = pl.BlockSpec((2, rank, hid), lambda i, meta: (0, 0, 0))
    return pl.pallas_call(
        functools.partial(cross_kernel, bool(before)),
        grid_spec=pltpu.PrefetchScalarGridSpec(
            num_scalar_prefetch=1,
            grid=(MOST,),
            in_specs=[sum_block, sum_block, row_block, other_block, row_block, other_block]
            + ([gram_spec, raw_spec] if before else []),
            out_specs=[gram_spec, raw_spec],
        ),
        out_shape=[
            jax.ShapeDtypeStruct((rank, rank), F32),
            jax.ShapeDtypeStruct((2, rank, hid), F32),
        ],
        compiler_params=params(),
        cost_estimate=cost(4 * MOST * rows * rank * (rank + 2 * hid), 8 * MOST * rows * rank * 3),
        name="crossed",
    )(meta, own, other, gate, gate, up, up, *before)


def project_kernel(count, *refs):
    tokens, sums, out, basis = refs[:count], refs[count:-2], refs[-2], refs[-1]
    rows = sums[0].shape[1]
    for i, ref in enumerate(sums):
        basis[i * rows : (i + 1) * rows, :] = ref[0]
    toks = tokens[0].shape[0]
    for i, ref in enumerate(tokens):
        out[i * toks : (i + 1) * toks, :] = mul(ref[:, LANES:], basis[...]).astype(BF16)


def project(tokens, sums, k):
    rank = sums[0].shape[-1]
    toks, width = tokens[0].shape
    depth = width - LANES
    total = len(tokens) * toks
    return pl.pallas_call(
        functools.partial(project_kernel, len(tokens)),
        grid=(1,),
        in_specs=[pl.BlockSpec((toks, width), lambda i: (0, 0))] * len(tokens)
        + [pl.BlockSpec((1,) + value.shape[1:], lambda i: (k, 0, 0)) for value in sums],
        out_specs=pl.BlockSpec((total, rank), lambda i: (0, 0)),
        out_shape=jax.ShapeDtypeStruct((total, rank), BF16),
        scratch_shapes=[pltpu.VMEM((depth, rank), BF16)],
        compiler_params=params(),
        cost_estimate=cost(2 * total * depth * rank, 4 * total * rank),
        name="project",
    )(*tokens, *sums)


def reciprocal(value):
    guess = pl.reciprocal(value, approx=True)
    guess = guess * (2.0 - value * guess)
    return guess * (2.0 - value * guess)


def factor_kernel(tile, gram_ref, raw_ref, inverse_ref, coeff_ref, work_ref):
    rank = gram_ref.shape[0]
    steps = rank // tile
    row_of = lax.broadcasted_iota(jnp.int32, (tile, tile), 0)
    col_of = lax.broadcasted_iota(jnp.int32, (tile, tile), 1)
    corners = [
        jnp.where(row_of == col_of, gram_ref[t * tile : (t + 1) * tile, t * tile : (t + 1) * tile], 0.0)
        for t in range(steps)
    ]
    scale = lax.rsqrt(
        jnp.concatenate([jnp.sum(c, axis=0, keepdims=True) for c in corners], axis=1)
    )
    for t in range(steps):
        strip = slice(t * tile, (t + 1) * tile)
        scale_rows = lax.rsqrt(jnp.sum(corners[t], axis=1, keepdims=True))
        work_ref[strip, :] = gram_ref[strip, :] * scale_rows * scale
    lane = lax.broadcasted_iota(jnp.int32, (8, tile), 1)
    sub = lax.broadcasted_iota(jnp.int32, (8, tile), 0)
    lane_row = lane[:1]

    def step(index, carry):
        base = pl.multiple_of(index * tile, tile)
        here = pl.ds(base, tile)
        strips = [
            work_ref[pl.ds(pl.multiple_of(base + 8 * s, 8), 8), here] for s in range(tile // 8)
        ]
        for j in range(0, tile, 2):
            first, inner = divmod(j, 8)
            both = strips[first]
            row0, row1 = both[inner : inner + 1, :], both[inner + 1 : inner + 2, :]
            a, b, d = row0[:, j : j + 1], row1[:, j : j + 1], row1[:, j + 1 : j + 2]
            inverse_a = reciprocal(a)
            inverse_d = a * reciprocal(a * d - b * b)
            ratio = b * inverse_a
            later = jnp.where(lane_row == j, 0.0, row1) - ratio * jnp.where(lane_row == j, 1.0, row0)
            scaled0 = jnp.where(lane_row == j, 1.0, row0) * inverse_a
            scaled1 = jnp.where(lane_row == j + 1, 1.0, later) * inverse_d
            for s in range(first, tile // 8):
                strip = strips[s]
                column0 = strip[:, j : j + 1]
                column1 = strip[:, j + 1 : j + 2] - column0 * ratio
                new = jnp.where((lane == j) | (lane == j + 1), 0.0, strip)
                new = new - column0 * jnp.where(lane_row == j + 1, 0.0, scaled0) - column1 * scaled1
                if s == first:
                    new = jnp.where(sub > inner + 1, new, jnp.where(sub == inner + 1, later, strip))
                strips[s] = new
        block = jnp.concatenate(strips, axis=0)
        pivots = jnp.sum(jnp.where(row_of == col_of, block, 0.0), axis=1, keepdims=True)
        unit = jnp.where(row_of == col_of, 1.0, 0.0)
        own = jnp.where(col_of < row_of, block, unit) / jnp.sqrt(pivots)
        work_ref[here, here] = unit
        right = exact(own, work_ref[here, :], ((1,), (0,)))
        columns = lax.broadcasted_iota(jnp.int32, (tile, rank), 1)
        inverse_ref[here, :] = jnp.where(columns < base + tile, right * scale, 0.0)
        for s in range(steps - 1):

            @pl.when(index == s)
            def _():
                below = slice((s + 1) * tile, rank)
                mine = slice(s * tile, (s + 1) * tile)
                left = exact(work_ref[below, mine], own, ((1,), (1,)))
                work_ref[below, mine] = jnp.zeros((rank - (s + 1) * tile, tile), F32)
                work_ref[below, :] = work_ref[below, :] - exact(left, right, ((1,), (0,)))

        return carry

    lax.fori_loop(0, steps, step, 0)
    inverse = inverse_ref[...]
    for side in range(2):
        coeff_ref[side] = mul3(inverse, raw_ref[side], ((1,), (0,))).astype(BF16)


def factored(gram, raw):
    rank = gram.shape[0]
    return pl.pallas_call(
        functools.partial(factor_kernel, min(LANES, rank)),
        out_shape=[
            jax.ShapeDtypeStruct((rank, rank), F32),
            jax.ShapeDtypeStruct(raw.shape, BF16),
        ],
        in_specs=[whole()] * 2,
        out_specs=[whole()] * 2,
        scratch_shapes=[pltpu.VMEM((rank, rank), F32)],
        compiler_params=params(),
        cost_estimate=cost(4e10, 8 * rank * rank),
        name="factored",
    )(gram, raw)


def hidden_kernel(toks, groups, meta, inverse, mine, others, tokens, *refs):
    arrived, outs = refs[:MOST], refs[MOST:]
    group = meta[2 * MOST] // MOST
    lane = lax.broadcasted_iota(jnp.int32, tokens.shape, 1)
    picked = (lane == group) | (lane == group + groups)
    share = jnp.sum(jnp.where(picked, tokens[...].astype(F32), 0.0), axis=1, keepdims=True)
    raw = []
    for k in range(MOST):
        total = jnp.zeros((toks, inverse.shape[0]), F32)
        for mask in range(MOST):
            source = (k ^ mask) * toks
            total += arrived[mask][source : source + toks, :].astype(F32)
        raw.append(total)
    projected = mul3(jnp.concatenate(raw, axis=0), inverse[...], ((1,), (1,))).astype(BF16)
    hid = mine.shape[2]
    for d, side in enumerate((mine, others)):
        gate = mul(projected, side[0])
        hidden = gate / (1.0 + jnp.exp(-gate)) * mul(projected, side[1]) * share
        hidden = hidden.astype(BF16)
        block = pl.ds(pl.multiple_of(meta[d * MOST] // MOST * hid, LANES), hid)
        for k in range(MOST):
            x, y = k % 2, k // 2
            rows = hidden[k * toks : (k + 1) * toks]
            outs[x][0, y * toks : (y + 1) * toks, block] = rows
            outs[2 + y][0, x * toks : (x + 1) * toks, block] = rows
        outs[4][0, :, block] = hidden


def hidden_rows(meta, inverse, coeff, other_coeff, tokens, arrived, toks):
    rank, hid = coeff.shape[1:]
    groups = tokens.shape[0] // (MOST * toks)
    block = MOST * toks
    out = jax.ShapeDtypeStruct((groups, block // 2, 2 * hid), BF16)
    coeff_spec = pl.BlockSpec((2, rank, hid), lambda g: (0, 0, 0))
    return pl.pallas_call(
        functools.partial(hidden_kernel, toks, groups),
        grid=(groups,),
        in_specs=[
            scalars(),
            pl.BlockSpec((rank, rank), lambda g: (0, 0)),
            coeff_spec,
            coeff_spec,
            pl.BlockSpec((block, LANES), lambda g: (g, 0)),
        ]
        + [pl.BlockSpec((block, rank), lambda g: (g, 0))] * MOST,
        out_specs=[pl.BlockSpec((1, block // 2, 2 * hid), lambda g: (g, 0, 0))] * 4
        + [pl.BlockSpec((1, block, 2 * hid), lambda g: (g, 0, 0))],
        out_shape=[out] * 4 + [jax.ShapeDtypeStruct((groups, block, 2 * hid), BF16)],
        compiler_params=params(),
        cost_estimate=cost(groups * block * rank * (6 * rank + 8 * hid), 16 * groups * block * hid),
        name="hidden_rows",
    )(meta, inverse, coeff, other_coeff, tokens, *arrived)


def group_masks(experts):
    masks, mask = [], MOST
    while mask < experts:
        masks.insert(0, mask)
        mask *= 2
    return masks


def column_chunks(depth, bits):
    near = list(range(bits - 1, 1, -1))
    orders = [[0, 1] + near, [1, 0] + near, near + [0, 1]]
    units = depth // LANES
    if units % 56:
        return [(0, depth, orders[0])]
    sizes = [(13, 0), (13, 1), (10, 2), (10, 0), (10, 1)]
    chunks, start = [], 0
    for size, order in sizes:
        width = size * (units // 56) * LANES
        chunks.append((start, width, orders[order]))
        start += width
    return chunks


def scattered_answers(sides, down, toks):
    experts = lax.axis_size("expert")
    masks = [1, 2] + group_masks(experts)
    bits = len(masks)
    chunks = column_chunks(down.shape[1], bits)
    groups = experts // MOST
    halves = {0: sides[0:2], 1: sides[2:4]}
    if groups > 1:
        halves[bits - 1] = (sides[4][: groups // 2], sides[4][groups // 2 :])

    def answered(rows, start, width):
        return mul(rows.reshape(-1, rows.shape[-1]), down[:, start : start + width])

    first = [
        swap_expert(answered(halves[order[0]][1], start, width).astype(BF16), masks[order[0]])
        for start, width, order in chunks
    ]
    values = [
        (answered(halves[order[0]][0], start, width) + came.astype(F32)).astype(BF16)
        for came, (start, width, order) in zip(first, chunks)
    ]
    left = [[bit for bit in range(bits - 1, -1, -1) if bit != order[0]] for _, _, order in chunks]
    for step in range(1, bits):
        for i, (_, width, order) in enumerate(chunks):
            bit = order[step]
            axis = left[i].index(bit)
            value = values[i].reshape((2,) * len(left[i]) + (toks, width))
            kept, out = (lax.index_in_dim(value, side, axis, keepdims=False) for side in (0, 1))
            values[i] = (kept.astype(F32) + swap_expert(out, masks[bit]).astype(F32)).astype(BF16)
            left[i].remove(bit)
    return jnp.concatenate([value.reshape(toks, -1) for value in values], axis=1)


def on_device(tokens, gate_weight, up_weight, down_weight, sketch, clusters, routes, route_weights):
    experts = lax.axis_size("expert")
    position = lax.axis_index("expert").astype(jnp.int32)
    place = position % MOST
    groups = experts // MOST
    half = lax.axis_index("dp").astype(jnp.int32)
    gate_rows = gate_weight[0]
    up_rows = up_weight[0]
    depth, rank = gate_rows.shape[0], sketch.shape[-1]
    rows = depth // 2 // MOST
    toks = tokens.shape[0]
    steps = jnp.arange(2 * MOST, dtype=jnp.int32)
    order = ((steps // MOST) ^ half) * MOST + ((steps % MOST) ^ place)
    meta = jnp.concatenate([order, position[None], clusters])

    down_rows = lax.all_gather(down_weight[0], "dp", axis=0, tiled=True)

    sent_half = swap_dp(sketch_half(meta, gate_rows, up_rows, sketch[0], 1, rows))
    own_half = sketch_half(meta, gate_rows, up_rows, sketch[0], 0, rows)
    pieces = token_pieces(meta, tokens, routes, route_weights, groups, rows, place)
    plane = [pieces[0]] + [swap_expert(pieces[k], k) for k in range(1, MOST)]
    spread = jnp.concatenate(plane, axis=0)
    spread, own_half = lax.optimization_barrier((spread, own_half))

    chunks = 2 if rows % 32 == 0 else 1
    chunk = rows // chunks
    got = []
    for c in range(chunks):
        span = slice(c * chunk, (c + 1) * chunk)
        own = [
            (own_half[k, span].astype(F32) + sent_half[k, span].astype(F32)).astype(BF16)
            for k in range(MOST)
        ]
        got.append([own[0]] + [swap_expert(own[k], k) for k in range(1, MOST)])
    group_sums, own_sums = [], []
    masks = group_masks(experts)
    for c in range(chunks):
        share = masks[c * len(masks) // chunks : (c + 1) * len(masks) // chunks]
        for mask in share[:-1]:
            spread = jnp.concatenate([spread, swap_expert(spread, mask)], axis=0)
        came = swap_expert(spread, share[-1]) if share else spread[:16]
        if c == 0:
            sums, mine, came = cluster_rows(meta, got[c], came)
        else:
            sums, mine, _ = cluster_rows(meta, got[c], meta)
        if share:
            spread = jnp.concatenate([spread, came], axis=0)
        group_sums.append((sums, swap_dp(sums)))
        own_sums.append((mine, swap_dp(mine)))
    halves = [sums[d] for d in range(2) for sums in group_sums]
    sends = {k: project([spread], halves, k) for k in (3, 1, 2, 0)}
    parts = [sends[k] for k in range(MOST)]
    before = ()
    for c in range(chunks):
        before = crossed(meta, *own_sums[c], gate_rows, up_rows, c, chunks, before)
    gram, raw = before
    if lax.axis_size("tensor") > 1:
        gram, raw = lax.psum((gram, raw), "tensor")
        parts = [lax.psum(value.astype(F32), "tensor").astype(BF16) for value in parts]
    gram, raw, parts = lax.optimization_barrier((gram, raw, parts))
    arrived = [parts[0]] + [swap_expert(parts[k], k) for k in range(1, MOST)]
    inverse, coeff = factored(gram, raw)
    other_coeff = swap_dp(coeff)
    shares = spread[:, :LANES]
    sides = hidden_rows(meta, inverse, coeff, other_coeff, shares, arrived, toks)
    return scattered_answers(sides, down_rows, toks)


def solution(mesh):
    return jax.shard_map(
        on_device,
        mesh=mesh,
        in_specs=(
            P(("expert", "dp"), "tensor"),
            P("expert", "tensor", "dp"),
            P("expert", "tensor", "dp"),
            P("expert", "dp", "tensor"),
            P("expert", None, "dp", None),
            P(),
            P(("expert", "dp"), None),
            P(("expert", "dp"), None),
        ),
        out_specs=P(("expert", "dp"), "tensor"),
        check_vma=False,
    )
```

```python
import functools

import jax
import jax.numpy as jnp
from jax import lax
from jax.experimental import pallas as pl
from jax.experimental.pallas import tpu as pltpu
from jax.sharding import PartitionSpec as P

MOST = 4
LANES = 128
VMEM_BYTES = 56 * 1024 * 1024

HIGHEST = lax.Precision.HIGHEST
F32 = jnp.float32
BF16 = jnp.bfloat16


def swap_expert(value, mask):
    count = lax.axis_size("expert")
    return lax.ppermute(value, "expert", [(source, source ^ mask) for source in range(count)])


def swap_dp(value):
    count = lax.axis_size("dp")
    return lax.ppermute(value, "dp", [(source, count - 1 - source) for source in range(count)])


def shift_groups(value, steps):
    count = lax.axis_size("expert")
    moves = [(s, s + steps) for s in range(count) if 0 <= s + steps < count]
    return lax.ppermute(value, "expert", moves)


def whole():
    return pl.BlockSpec(memory_space=pltpu.VMEM)


def scalars():
    return pl.BlockSpec(memory_space=pltpu.SMEM)


def params(**more):
    return pltpu.CompilerParams(vmem_limit_bytes=VMEM_BYTES, **more)


def cost(flops, moved):
    return pl.CostEstimate(flops=int(flops), bytes_accessed=int(moved), transcendentals=0)


def mul(a, b, dims=((1,), (0,))):
    return lax.dot_general(a, b, (dims, ((), ())), preferred_element_type=F32)


def exact(a, b, dims):
    return lax.dot_general(a, b, (dims, ((), ())), precision=HIGHEST, preferred_element_type=F32)


def parts_of(value):
    high = value.astype(BF16)
    return high, (value - high.astype(F32)).astype(BF16)


def mul3(a, b, dims):
    (a0, a1), (b0, b1) = parts_of(a), parts_of(b)
    return mul(a0, b0, dims) + (mul(a0, b1, dims) + mul(a1, b0, dims))


def token_kernel(groups, rows, meta, tokens, routes, weights, *pieces):
    place = lax.rem(meta[2 * MOST], MOST)
    toks = tokens.shape[0]
    lane = lax.broadcasted_iota(jnp.int32, (toks, LANES), 1)
    group = lax.rem(lane, groups)
    for k in range(MOST):
        expert = group * MOST + (place ^ k)
        share = jnp.zeros((toks, LANES), F32)
        for t in range(routes.shape[1]):
            share += jnp.where(routes[:, t : t + 1] == expert, weights[:, t : t + 1], 0.0)
        high, low = parts_of(share)
        pieces[k][:, :LANES] = jnp.where(
            lane < groups, high.astype(F32), low.astype(F32)
        ).astype(BF16)
        for d in range(2):
            start = pl.multiple_of(meta[d * MOST + k] * rows, LANES)
            pieces[k][:, LANES + d * rows : LANES + (d + 1) * rows] = tokens[:, pl.ds(start, rows)]


def token_pieces(meta, tokens, routes, weights, groups, rows, place):
    toks = tokens.shape[0]
    if rows % LANES == 0:
        return pl.pallas_call(
            functools.partial(token_kernel, groups, rows),
            out_shape=[jax.ShapeDtypeStruct((toks, LANES + 2 * rows), BF16)] * MOST,
            in_specs=[scalars(), whole(), whole(), whole()],
            out_specs=[whole()] * MOST,
            compiler_params=params(),
            name="token_pieces",
        )(meta, tokens, routes, weights)
    lane = jnp.arange(LANES, dtype=jnp.int32)
    pieces = []
    for k in range(MOST):
        expert = (lane % groups) * MOST + (place ^ k)
        share = jnp.sum(jnp.where(routes[:, :, None] == expert, weights[:, :, None], 0.0), axis=1)
        high, low = parts_of(share)
        columns = [
            lax.dynamic_slice_in_dim(tokens, meta[d * MOST + k] * rows, rows, axis=1)
            for d in range(2)
        ]
        pieces.append(jnp.concatenate([jnp.where(lane < groups, high, low)] + columns, axis=1))
    return pieces


def sketch_kernel(meta, gate, up, sketch, out):
    both = jnp.concatenate([gate[...], up[...]], axis=1)
    out[0] = mul(both, jnp.concatenate([sketch[0], sketch[1]], axis=0)).astype(BF16)


def sketch_half(meta, gate, up, sketch, side, rows):
    hid, rank = sketch.shape[1:]
    row_block = pl.BlockSpec((rows, hid), lambda k, meta: (meta[side * MOST + k], 0))
    return pl.pallas_call(
        sketch_kernel,
        grid_spec=pltpu.PrefetchScalarGridSpec(
            num_scalar_prefetch=1,
            grid=(MOST,),
            in_specs=[row_block, row_block, pl.BlockSpec((2, hid, rank), lambda k, meta: (0, 0, 0))],
            out_specs=pl.BlockSpec((1, rows, rank), lambda k, meta: (k, 0, 0)),
        ),
        out_shape=jax.ShapeDtypeStruct((MOST, rows, rank), BF16),
        compiler_params=params(),
        cost_estimate=cost(4 * MOST * rows * hid * rank, 4 * MOST * rows * hid),
        name="sketch_half",
    )(meta, gate, up, sketch)


def chosen(values, names, name):
    total = jnp.zeros(values[0].shape, F32)
    for value, own in zip(values, names):
        total += jnp.where(own == name, value, 0.0)
    return total


def ends_kernel(meta, *refs):
    values = [ref[...].astype(F32) for ref in refs[:MOST]]
    tail, head = refs[MOST:]
    position = meta[2 * MOST]
    place = lax.rem(position, MOST)
    first = position - place
    base = 2 * MOST + 1
    names = [meta[base + first + (place ^ k)] for k in range(MOST)]
    tail[...] = chosen(values, names, meta[base + first + MOST - 1]).astype(BF16)
    head[...] = chosen(values, names, meta[base + first]).astype(BF16)


def totals_kernel(experts, meta, *refs):
    values = [ref[...].astype(F32) for ref in refs[:MOST]]
    below, above = (ref[...].astype(F32) for ref in refs[MOST : MOST + 2])
    stacked, sends = refs[MOST + 2], refs[MOST + 3 :]
    position = meta[2 * MOST]
    place = lax.rem(position, MOST)
    first = position - place
    base = 2 * MOST + 1
    names = [meta[base + first + (place ^ k)] for k in range(MOST)]
    below_name = jnp.where(first > 0, meta[base + jnp.maximum(first - 1, 0)], -1)
    above_name = jnp.where(
        first + MOST < experts, meta[base + jnp.minimum(first + MOST, experts - 1)], -1
    )
    for k in range(MOST):
        total = chosen(values, names, names[k])
        total += jnp.where(names[k] == below_name, below, 0.0)
        total += jnp.where(names[k] == above_name, above, 0.0)
        total = total.astype(BF16)
        stacked[k] = total
        if k:
            sends[k - 1][...] = total


def stack_kernel(*refs):
    for k in range(MOST):
        refs[MOST][k] = refs[k][...]


def group_sums(meta, got):
    shape = got[0].shape
    experts = lax.axis_size("expert")
    piece = jax.ShapeDtypeStruct(shape, BF16)
    tail, head = pl.pallas_call(
        ends_kernel,
        out_shape=[piece, piece],
        in_specs=[scalars()] + [whole()] * MOST,
        out_specs=[whole()] * 2,
        compiler_params=params(),
        name="end_sums",
    )(meta, *got)
    below = shift_groups(tail, MOST)
    above = shift_groups(head, -MOST)
    return pl.pallas_call(
        functools.partial(totals_kernel, experts),
        out_shape=[jax.ShapeDtypeStruct((MOST,) + shape, BF16)] + [piece] * (MOST - 1),
        in_specs=[scalars()] + [whole()] * (MOST + 2),
        out_specs=[whole()] * MOST,
        compiler_params=params(),
        name="cluster_sums",
    )(meta, *got, below, above)


def stacked(values):
    return pl.pallas_call(
        stack_kernel,
        out_shape=jax.ShapeDtypeStruct((MOST,) + values[0].shape, BF16),
        in_specs=[whole()] * MOST,
        out_specs=whole(),
        compiler_params=params(),
        name="own_sums",
    )(*values)


def cross_kernel(started, meta, own, other, gate, gate_other, up, up_other, *refs):
    if started:
        old_gram, old_raw, gram, raw = refs
    else:
        gram, raw = refs
    step = pl.program_id(0)

    @pl.when(step == 0)
    def _():
        gram[...] = old_gram[...] if started else jnp.zeros(gram.shape, F32)
        raw[...] = old_raw[...] if started else jnp.zeros(raw.shape, F32)

    rows = jnp.concatenate([own[0], other[0]], axis=0)
    turned = rows.T
    gram[...] += mul(turned, rows)
    raw[0] += mul(turned, jnp.concatenate([gate[...], gate_other[...]], axis=0))
    raw[1] += mul(turned, jnp.concatenate([up[...], up_other[...]], axis=0))


def crossed(meta, own, other, gate, up, chunk, chunks, before):
    _, rows, rank = own.shape
    hid = gate.shape[1]
    sum_block = pl.BlockSpec((1, rows, rank), lambda i, meta: (i, 0, 0))
    row_block = pl.BlockSpec((rows, hid), lambda i, meta: (meta[i] * chunks + chunk, 0))
    other_block = pl.BlockSpec((rows, hid), lambda i, meta: (meta[MOST + i] * chunks + chunk, 0))
    gram_spec = pl.BlockSpec((rank, rank), lambda i, meta: (0, 0))
    raw_spec = pl.BlockSpec((2, rank, hid), lambda i, meta: (0, 0, 0))
    return pl.pallas_call(
        functools.partial(cross_kernel, bool(before)),
        grid_spec=pltpu.PrefetchScalarGridSpec(
            num_scalar_prefetch=1,
            grid=(MOST,),
            in_specs=[sum_block, sum_block, row_block, other_block, row_block, other_block]
            + ([gram_spec, raw_spec] if before else []),
            out_specs=[gram_spec, raw_spec],
        ),
        out_shape=[
            jax.ShapeDtypeStruct((rank, rank), F32),
            jax.ShapeDtypeStruct((2, rank, hid), F32),
        ],
        compiler_params=params(),
        cost_estimate=cost(4 * MOST * rows * rank * (rank + 2 * hid), 8 * MOST * rows * rank * 3),
        name="crossed",
    )(meta, own, other, gate, gate, up, up, *before)


def project_kernel(count, tokens, *refs):
    sums, outs, basis = refs[:count], refs[count:-1], refs[-1]
    rows = sums[0].shape[1]
    for i, ref in enumerate(sums):
        basis[i * rows : (i + 1) * rows, :] = ref[0]
    toks = tokens.shape[0] // MOST
    for k in range(MOST):

        @pl.when(pl.program_id(0) == k)
        def _():
            for i in range(MOST):
                strip = slice(i * toks, (i + 1) * toks)
                outs[k][strip, :] = mul(tokens[strip, LANES:], basis[...]).astype(BF16)


def project(tokens, sums):
    rank = sums[0].shape[-1]
    total, width = tokens.shape
    depth = width - LANES
    return pl.pallas_call(
        functools.partial(project_kernel, len(sums)),
        grid=(MOST,),
        in_specs=[pl.BlockSpec((total, width), lambda k: (0, 0))]
        + [pl.BlockSpec((1,) + value.shape[1:], lambda k: (k, 0, 0)) for value in sums],
        out_specs=[pl.BlockSpec((total, rank), lambda k: (0, 0))] * MOST,
        out_shape=[jax.ShapeDtypeStruct((total, rank), BF16)] * MOST,
        scratch_shapes=[pltpu.VMEM((depth, rank), BF16)],
        compiler_params=params(),
        cost_estimate=cost(2 * MOST * total * depth * rank, 4 * MOST * total * rank),
        name="project",
    )(tokens, *sums)


def reciprocal(value):
    guess = pl.reciprocal(value, approx=True)
    guess = guess * (2.0 - value * guess)
    return guess * (2.0 - value * guess)


def factor_kernel(tile, gram_ref, inverse_ref, work_ref):
    rank = gram_ref.shape[0]
    steps = rank // tile
    row_of = lax.broadcasted_iota(jnp.int32, (tile, tile), 0)
    col_of = lax.broadcasted_iota(jnp.int32, (tile, tile), 1)
    corners = [
        jnp.where(row_of == col_of, gram_ref[t * tile : (t + 1) * tile, t * tile : (t + 1) * tile], 0.0)
        for t in range(steps)
    ]
    scale = lax.rsqrt(
        jnp.concatenate([jnp.sum(c, axis=0, keepdims=True) for c in corners], axis=1)
    )
    for t in range(steps):
        strip = slice(t * tile, (t + 1) * tile)
        scale_rows = lax.rsqrt(jnp.sum(corners[t], axis=1, keepdims=True))
        work_ref[strip, :] = gram_ref[strip, :] * scale_rows * scale
    lane = lax.broadcasted_iota(jnp.int32, (8, tile), 1)
    sub = lax.broadcasted_iota(jnp.int32, (8, tile), 0)
    lane_row = lane[:1]

    def step(index, carry):
        base = pl.multiple_of(index * tile, tile)
        here = pl.ds(base, tile)
        strips = [
            work_ref[pl.ds(pl.multiple_of(base + 8 * s, 8), 8), here] for s in range(tile // 8)
        ]
        for j in range(0, tile, 2):
            first, inner = divmod(j, 8)
            both = strips[first]
            row0, row1 = both[inner : inner + 1, :], both[inner + 1 : inner + 2, :]
            a, b, d = row0[:, j : j + 1], row1[:, j : j + 1], row1[:, j + 1 : j + 2]
            inverse_a = reciprocal(a)
            inverse_d = a * reciprocal(a * d - b * b)
            ratio = b * inverse_a
            later = jnp.where(lane_row == j, 0.0, row1) - ratio * jnp.where(lane_row == j, 1.0, row0)
            scaled0 = jnp.where(lane_row == j, 1.0, row0) * inverse_a
            scaled1 = jnp.where(lane_row == j + 1, 1.0, later) * inverse_d
            for s in range(first, tile // 8):
                strip = strips[s]
                column0 = strip[:, j : j + 1]
                column1 = strip[:, j + 1 : j + 2] - column0 * ratio
                new = jnp.where((lane == j) | (lane == j + 1), 0.0, strip)
                new = new - column0 * jnp.where(lane_row == j + 1, 0.0, scaled0) - column1 * scaled1
                if s == first:
                    new = jnp.where(sub > inner + 1, new, jnp.where(sub == inner + 1, later, strip))
                strips[s] = new
        block = jnp.concatenate(strips, axis=0)
        pivots = jnp.sum(jnp.where(row_of == col_of, block, 0.0), axis=1, keepdims=True)
        unit = jnp.where(row_of == col_of, 1.0, 0.0)
        own = jnp.where(col_of < row_of, block, unit) / jnp.sqrt(pivots)
        work_ref[here, here] = unit
        right = exact(own, work_ref[here, :], ((1,), (0,)))
        columns = lax.broadcasted_iota(jnp.int32, (tile, rank), 1)
        inverse_ref[here, :] = jnp.where(columns < base + tile, right * scale, 0.0)
        for s in range(steps - 1):

            @pl.when(index == s)
            def _():
                below = slice((s + 1) * tile, rank)
                mine = slice(s * tile, (s + 1) * tile)
                left = exact(work_ref[below, mine], own, ((1,), (1,)))
                work_ref[below, mine] = jnp.zeros((rank - (s + 1) * tile, tile), F32)
                work_ref[below, :] = work_ref[below, :] - exact(left, right, ((1,), (0,)))

        return carry

    lax.fori_loop(0, steps, step, 0)


def factored(gram):
    rank = gram.shape[0]
    return pl.pallas_call(
        functools.partial(factor_kernel, min(LANES, rank)),
        out_shape=jax.ShapeDtypeStruct((rank, rank), F32),
        in_specs=[whole()],
        out_specs=whole(),
        scratch_shapes=[pltpu.VMEM((rank, rank), F32)],
        compiler_params=params(),
        cost_estimate=cost(4e10, 8 * rank * rank),
        name="factored",
    )(gram)


def coefficient_kernel(inverse, raw, out):
    out[0] = mul3(inverse[...], raw[0], ((1,), (0,))).astype(BF16)


def coefficients(inverse, raw):
    sides, rank, hid = raw.shape
    side = pl.BlockSpec((1, rank, hid), lambda i: (i, 0, 0))
    return pl.pallas_call(
        coefficient_kernel,
        grid=(sides,),
        in_specs=[pl.BlockSpec((rank, rank), lambda i: (0, 0)), side],
        out_specs=side,
        out_shape=jax.ShapeDtypeStruct(raw.shape, BF16),
        compiler_params=params(),
        cost_estimate=cost(6 * sides * rank * rank * hid, 6 * sides * rank * hid),
        name="coefficients",
    )(inverse, raw)


def hidden_kernel(toks, groups, meta, inverse, mine, others, tokens, *refs):
    arrived, outs = refs[:MOST], refs[MOST:]
    group = meta[2 * MOST] // MOST
    lane = lax.broadcasted_iota(jnp.int32, tokens.shape, 1)
    picked = (lane == group) | (lane == group + groups)
    share = jnp.sum(jnp.where(picked, tokens[...].astype(F32), 0.0), axis=1, keepdims=True)
    raw = []
    for k in range(MOST):
        total = jnp.zeros((toks, inverse.shape[0]), F32)
        for mask in range(MOST):
            source = (k ^ mask) * toks
            total += arrived[mask][source : source + toks, :].astype(F32)
        raw.append(total)
    projected = mul3(jnp.concatenate(raw, axis=0), inverse[...], ((1,), (1,))).astype(BF16)
    hid = mine.shape[2]
    for d, side in enumerate((mine, others)):
        gate = mul(projected, side[0])
        hidden = gate / (1.0 + jnp.exp(-gate)) * mul(projected, side[1]) * share
        hidden = hidden.astype(BF16)
        block = pl.ds(pl.multiple_of(meta[d * MOST] // MOST * hid, LANES), hid)
        for k in range(MOST):
            x, y = k % 2, k // 2
            rows = hidden[k * toks : (k + 1) * toks]
            outs[x][0, y * toks : (y + 1) * toks, block] = rows
            outs[2 + y][0, x * toks : (x + 1) * toks, block] = rows
        outs[4][0, :, block] = hidden


def hidden_rows(meta, inverse, coeff, other_coeff, tokens, arrived, toks):
    rank, hid = coeff.shape[1:]
    groups = tokens.shape[0] // (MOST * toks)
    block = MOST * toks
    out = jax.ShapeDtypeStruct((groups, block // 2, 2 * hid), BF16)
    coeff_spec = pl.BlockSpec((2, rank, hid), lambda g: (0, 0, 0))
    return pl.pallas_call(
        functools.partial(hidden_kernel, toks, groups),
        grid=(groups,),
        in_specs=[
            scalars(),
            pl.BlockSpec((rank, rank), lambda g: (0, 0)),
            coeff_spec,
            coeff_spec,
            pl.BlockSpec((block, LANES), lambda g: (g, 0)),
        ]
        + [pl.BlockSpec((block, rank), lambda g: (g, 0))] * MOST,
        out_specs=[pl.BlockSpec((1, block // 2, 2 * hid), lambda g: (g, 0, 0))] * 4
        + [pl.BlockSpec((1, block, 2 * hid), lambda g: (g, 0, 0))],
        out_shape=[out] * 4 + [jax.ShapeDtypeStruct((groups, block, 2 * hid), BF16)],
        compiler_params=params(),
        cost_estimate=cost(groups * block * rank * (6 * rank + 8 * hid), 16 * groups * block * hid),
        name="hidden_rows",
    )(meta, inverse, coeff, other_coeff, tokens, *arrived)


def group_masks(experts):
    masks, mask = [], MOST
    while mask < experts:
        masks.insert(0, mask)
        mask *= 2
    return masks


def column_chunks(depth, bits):
    near = list(range(bits - 1, 1, -1))
    orders = [[0, 1] + near, [1, 0] + near, near + [0, 1]]
    units = depth // LANES
    if units % 56:
        return [(0, depth, orders[0])]
    sizes = [(11, 0), (11, 1), (12, 2), (11, 0), (11, 1)]
    chunks, start = [], 0
    for size, order in sizes:
        width = size * (units // 56) * LANES
        chunks.append((start, width, orders[order]))
        start += width
    return chunks


def scattered_answers(sides, down, toks):
    experts = lax.axis_size("expert")
    masks = [1, 2] + group_masks(experts)
    bits = len(masks)
    chunks = column_chunks(down.shape[1], bits)
    groups = experts // MOST
    halves = {0: sides[0:2], 1: sides[2:4]}
    if groups > 1:
        halves[bits - 1] = (sides[4][: groups // 2], sides[4][groups // 2 :])

    def answered(rows, start, width):
        return mul(rows.reshape(-1, rows.shape[-1]), down[:, start : start + width])

    first = [
        swap_expert(answered(halves[order[0]][1], start, width).astype(BF16), masks[order[0]])
        for start, width, order in chunks
    ]
    values = [
        (answered(halves[order[0]][0], start, width) + came.astype(F32)).astype(BF16)
        for came, (start, width, order) in zip(first, chunks)
    ]
    left = [[bit for bit in range(bits - 1, -1, -1) if bit != order[0]] for _, _, order in chunks]
    for step in range(1, bits):
        for i, (_, width, order) in enumerate(chunks):
            bit = order[step]
            axis = left[i].index(bit)
            value = values[i].reshape((2,) * len(left[i]) + (toks, width))
            kept, out = (lax.index_in_dim(value, side, axis, keepdims=False) for side in (0, 1))
            values[i] = (kept.astype(F32) + swap_expert(out, masks[bit]).astype(F32)).astype(BF16)
            left[i].remove(bit)
    return jnp.concatenate([value.reshape(toks, -1) for value in values], axis=1)


def on_device(tokens, gate_weight, up_weight, down_weight, sketch, clusters, routes, route_weights):
    experts = lax.axis_size("expert")
    position = lax.axis_index("expert").astype(jnp.int32)
    place = position % MOST
    groups = experts // MOST
    half = lax.axis_index("dp").astype(jnp.int32)
    gate_rows = gate_weight[0]
    up_rows = up_weight[0]
    depth, rank = gate_rows.shape[0], sketch.shape[-1]
    rows = depth // 2 // MOST
    toks = tokens.shape[0]
    steps = jnp.arange(2 * MOST, dtype=jnp.int32)
    order = ((steps // MOST) ^ half) * MOST + ((steps % MOST) ^ place)
    meta = jnp.concatenate([order, position[None], clusters])

    down_rows = lax.all_gather(down_weight[0], "dp", axis=0, tiled=True)

    sent_half = swap_dp(sketch_half(meta, gate_rows, up_rows, sketch[0], 1, rows))
    own_half = sketch_half(meta, gate_rows, up_rows, sketch[0], 0, rows)
    pieces = token_pieces(meta, tokens, routes, route_weights, groups, rows, place)
    plane = [pieces[0]] + [swap_expert(pieces[k], k) for k in range(1, MOST)]
    spread = jnp.concatenate(plane, axis=0)
    spread, own_half = lax.optimization_barrier((spread, own_half))

    chunks = 2 if rows % 32 == 0 else 1
    chunk = rows // chunks
    got = []
    for c in range(chunks):
        span = slice(c * chunk, (c + 1) * chunk)
        own = [
            (own_half[k, span].astype(F32) + sent_half[k, span].astype(F32)).astype(BF16)
            for k in range(MOST)
        ]
        got.append([own[0]] + [swap_expert(own[k], k) for k in range(1, MOST)])
    masks = group_masks(experts)
    for mask in masks[:-1]:
        spread = jnp.concatenate([spread, swap_expert(spread, mask)], axis=0)
    spread, got[0] = lax.optimization_barrier((spread, got[0]))
    if masks:
        spread = jnp.concatenate([spread, swap_expert(spread, masks[-1])], axis=0)
    sums, other_sums, back = [], [], []
    for c in range(chunks):
        value, *sends = group_sums(meta, got[c])
        sums.append(value)
        other_sums.append(swap_dp(value))
        back.append([value[0]] + [swap_expert(sends[k - 1], k) for k in range(1, MOST)])
    parts = project(spread, sums + other_sums)
    before = ()
    for c in range(chunks):
        if c == chunks - 1:
            parts, before, back[c] = lax.optimization_barrier((parts, before, back[c]))
        mine = stacked(back[c])
        before = crossed(meta, mine, swap_dp(mine), gate_rows, up_rows, c, chunks, before)
    gram, raw = before
    if lax.axis_size("tensor") > 1:
        gram, raw = lax.psum((gram, raw), "tensor")
        parts = [lax.psum(value.astype(F32), "tensor").astype(BF16) for value in parts]
    arrived = [parts[0]] + [swap_expert(parts[k], k) for k in range(1, MOST)]
    inverse = factored(gram)
    inverse, arrived = lax.optimization_barrier((inverse, arrived))
    coeff = coefficients(inverse, raw)
    other_coeff = swap_dp(coeff)
    shares = spread[:, :LANES]
    sides = hidden_rows(meta, inverse, coeff, other_coeff, shares, arrived, toks)
    return scattered_answers(sides, down_rows, toks)


def solution(mesh):
    return jax.shard_map(
        on_device,
        mesh=mesh,
        in_specs=(
            P(("expert", "dp"), "tensor"),
            P("expert", "tensor", "dp"),
            P("expert", "tensor", "dp"),
            P("expert", "dp", "tensor"),
            P("expert", None, "dp", None),
            P(),
            P(("expert", "dp"), None),
            P(("expert", "dp"), None),
        ),
        out_specs=P(("expert", "dp"), "tensor"),
        check_vma=False,
    )
```

```python
import functools

import jax
import jax.numpy as jnp
from jax import lax
from jax.experimental import pallas as pl
from jax.experimental.pallas import tpu as pltpu
from jax.sharding import PartitionSpec as P

MOST = 4
LANES = 128
VMEM_BYTES = 56 * 1024 * 1024

HIGHEST = lax.Precision.HIGHEST
F32 = jnp.float32
BF16 = jnp.bfloat16


def swap_expert(value, mask):
    count = lax.axis_size("expert")
    return lax.ppermute(value, "expert", [(source, source ^ mask) for source in range(count)])


def swap_dp(value):
    count = lax.axis_size("dp")
    return lax.ppermute(value, "dp", [(source, count - 1 - source) for source in range(count)])


def shift_groups(value, steps):
    count = lax.axis_size("expert")
    moves = [(s, s + steps) for s in range(count) if 0 <= s + steps < count]
    return lax.ppermute(value, "expert", moves)


def whole():
    return pl.BlockSpec(memory_space=pltpu.VMEM)


def scalars():
    return pl.BlockSpec(memory_space=pltpu.SMEM)


def params(**more):
    return pltpu.CompilerParams(vmem_limit_bytes=VMEM_BYTES, **more)


def cost(flops, moved):
    return pl.CostEstimate(flops=int(flops), bytes_accessed=int(moved), transcendentals=0)


def mul(a, b, dims=((1,), (0,))):
    return lax.dot_general(a, b, (dims, ((), ())), preferred_element_type=F32)


def exact(a, b, dims):
    return lax.dot_general(a, b, (dims, ((), ())), precision=HIGHEST, preferred_element_type=F32)


def parts_of(value):
    high = value.astype(BF16)
    return high, (value - high.astype(F32)).astype(BF16)


def mul3(a, b, dims):
    (a0, a1), (b0, b1) = parts_of(a), parts_of(b)
    return mul(a0, b0, dims) + (mul(a0, b1, dims) + mul(a1, b0, dims))


def token_kernel(groups, rows, meta, tokens, routes, weights, *pieces):
    place = lax.rem(meta[2 * MOST], MOST)
    toks = tokens.shape[0]
    lane = lax.broadcasted_iota(jnp.int32, (toks, LANES), 1)
    group = lax.rem(lane, groups)
    for k in range(MOST):
        expert = group * MOST + (place ^ k)
        share = jnp.zeros((toks, LANES), F32)
        for t in range(routes.shape[1]):
            share += jnp.where(routes[:, t : t + 1] == expert, weights[:, t : t + 1], 0.0)
        high, low = parts_of(share)
        pieces[k][:, :LANES] = jnp.where(
            lane < groups, high.astype(F32), low.astype(F32)
        ).astype(BF16)
        for d in range(2):
            start = pl.multiple_of(meta[d * MOST + k] * rows, LANES)
            pieces[k][:, LANES + d * rows : LANES + (d + 1) * rows] = tokens[:, pl.ds(start, rows)]


def token_pieces(meta, tokens, routes, weights, groups, rows, place):
    toks = tokens.shape[0]
    if rows % LANES == 0:
        return pl.pallas_call(
            functools.partial(token_kernel, groups, rows),
            out_shape=[jax.ShapeDtypeStruct((toks, LANES + 2 * rows), BF16)] * MOST,
            in_specs=[scalars(), whole(), whole(), whole()],
            out_specs=[whole()] * MOST,
            compiler_params=params(),
            name="token_pieces",
        )(meta, tokens, routes, weights)
    lane = jnp.arange(LANES, dtype=jnp.int32)
    pieces = []
    for k in range(MOST):
        expert = (lane % groups) * MOST + (place ^ k)
        share = jnp.sum(jnp.where(routes[:, :, None] == expert, weights[:, :, None], 0.0), axis=1)
        high, low = parts_of(share)
        columns = [
            lax.dynamic_slice_in_dim(tokens, meta[d * MOST + k] * rows, rows, axis=1)
            for d in range(2)
        ]
        pieces.append(jnp.concatenate([jnp.where(lane < groups, high, low)] + columns, axis=1))
    return pieces


def sketch_kernel(meta, gate, up, sketch, out):
    both = jnp.concatenate([gate[...], up[...]], axis=1)
    out[0] = mul(both, jnp.concatenate([sketch[0], sketch[1]], axis=0)).astype(BF16)


def sketch_half(meta, gate, up, sketch, side, rows):
    hid, rank = sketch.shape[1:]
    row_block = pl.BlockSpec((rows, hid), lambda k, meta: (meta[side * MOST + k], 0))
    return pl.pallas_call(
        sketch_kernel,
        grid_spec=pltpu.PrefetchScalarGridSpec(
            num_scalar_prefetch=1,
            grid=(MOST,),
            in_specs=[row_block, row_block, pl.BlockSpec((2, hid, rank), lambda k, meta: (0, 0, 0))],
            out_specs=pl.BlockSpec((1, rows, rank), lambda k, meta: (k, 0, 0)),
        ),
        out_shape=jax.ShapeDtypeStruct((MOST, rows, rank), BF16),
        compiler_params=params(),
        cost_estimate=cost(4 * MOST * rows * hid * rank, 4 * MOST * rows * hid),
        name="sketch_half",
    )(meta, gate, up, sketch)


def chosen(values, names, name):
    total = jnp.zeros(values[0].shape, F32)
    for value, own in zip(values, names):
        total += jnp.where(own == name, value, 0.0)
    return total


def ends_kernel(meta, *refs):
    values = [ref[...].astype(F32) for ref in refs[:MOST]]
    tail, head = refs[MOST:]
    position = meta[2 * MOST]
    place = lax.rem(position, MOST)
    first = position - place
    base = 2 * MOST + 1
    names = [meta[base + first + (place ^ k)] for k in range(MOST)]
    tail[...] = chosen(values, names, meta[base + first + MOST - 1]).astype(BF16)
    head[...] = chosen(values, names, meta[base + first]).astype(BF16)


def totals_kernel(experts, chunks, meta, *refs):
    values = [ref[...].astype(F32) for ref in refs[:MOST]]
    below, above = (ref[...].astype(F32) for ref in refs[MOST : MOST + 2])
    stacked, sends = refs[MOST + 2], refs[MOST + 3 :]
    position = meta[2 * MOST]
    place = lax.rem(position, MOST)
    first = position - place
    base = 2 * MOST + 1
    names = [meta[base + first + (place ^ k)] for k in range(MOST)]
    below_name = jnp.where(first > 0, meta[base + jnp.maximum(first - 1, 0)], -1)
    above_name = jnp.where(
        first + MOST < experts, meta[base + jnp.minimum(first + MOST, experts - 1)], -1
    )
    for k in range(MOST):
        total = chosen(values, names, names[k])
        total += jnp.where(names[k] == below_name, below, 0.0)
        total += jnp.where(names[k] == above_name, above, 0.0)
        total = total.astype(BF16)
        stacked[k] = total
        if k:
            for c in range(chunks):
                part = sends[c * (MOST - 1) + k - 1]
                rows = part.shape[0]
                part[...] = total[c * rows : (c + 1) * rows]


def stack_kernel(*refs):
    for k in range(MOST):
        refs[MOST][k] = refs[k][...]


def group_sums(meta, got, chunks):
    shape = got[0].shape
    experts = lax.axis_size("expert")
    piece = jax.ShapeDtypeStruct(shape, BF16)
    part = jax.ShapeDtypeStruct((shape[0] // chunks, shape[1]), BF16)
    tail, head = pl.pallas_call(
        ends_kernel,
        out_shape=[piece, piece],
        in_specs=[scalars()] + [whole()] * MOST,
        out_specs=[whole()] * 2,
        compiler_params=params(),
        name="end_sums",
    )(meta, *got)
    below = shift_groups(tail, MOST)
    above = shift_groups(head, -MOST)
    return pl.pallas_call(
        functools.partial(totals_kernel, experts, chunks),
        out_shape=[jax.ShapeDtypeStruct((MOST,) + shape, BF16)] + [part] * (chunks * (MOST - 1)),
        in_specs=[scalars()] + [whole()] * (MOST + 2),
        out_specs=[whole()] * (1 + chunks * (MOST - 1)),
        compiler_params=params(),
        name="cluster_sums",
    )(meta, *got, below, above)


def stacked(values):
    return pl.pallas_call(
        stack_kernel,
        out_shape=jax.ShapeDtypeStruct((MOST,) + values[0].shape, BF16),
        in_specs=[whole()] * MOST,
        out_specs=whole(),
        compiler_params=params(),
        name="own_sums",
    )(*values)


def cross_kernel(started, meta, own, other, gate, gate_other, up, up_other, *refs):
    if started:
        old_gram, old_raw, gram, raw = refs
    else:
        gram, raw = refs
    step = pl.program_id(0)

    @pl.when(step == 0)
    def _():
        gram[...] = old_gram[...] if started else jnp.zeros(gram.shape, F32)
        raw[...] = old_raw[...] if started else jnp.zeros(raw.shape, F32)

    rows = jnp.concatenate([own[0], other[0]], axis=0)
    turned = rows.T
    gram[...] += mul(turned, rows)
    raw[0] += mul(turned, jnp.concatenate([gate[...], gate_other[...]], axis=0))
    raw[1] += mul(turned, jnp.concatenate([up[...], up_other[...]], axis=0))


def crossed(meta, own, other, gate, up, chunk, chunks, before):
    _, rows, rank = own.shape
    hid = gate.shape[1]
    sum_block = pl.BlockSpec((1, rows, rank), lambda i, meta: (i, 0, 0))
    row_block = pl.BlockSpec((rows, hid), lambda i, meta: (meta[i] * chunks + chunk, 0))
    other_block = pl.BlockSpec((rows, hid), lambda i, meta: (meta[MOST + i] * chunks + chunk, 0))
    gram_spec = pl.BlockSpec((rank, rank), lambda i, meta: (0, 0))
    raw_spec = pl.BlockSpec((2, rank, hid), lambda i, meta: (0, 0, 0))
    return pl.pallas_call(
        functools.partial(cross_kernel, bool(before)),
        grid_spec=pltpu.PrefetchScalarGridSpec(
            num_scalar_prefetch=1,
            grid=(MOST,),
            in_specs=[sum_block, sum_block, row_block, other_block, row_block, other_block]
            + ([gram_spec, raw_spec] if before else []),
            out_specs=[gram_spec, raw_spec],
        ),
        out_shape=[
            jax.ShapeDtypeStruct((rank, rank), F32),
            jax.ShapeDtypeStruct((2, rank, hid), F32),
        ],
        compiler_params=params(),
        cost_estimate=cost(4 * MOST * rows * rank * (rank + 2 * hid), 8 * MOST * rows * rank * 3),
        name="crossed",
    )(meta, own, other, gate, gate, up, up, *before)


def project_kernel(count, tokens, *refs):
    sums, outs, basis = refs[:count], refs[count:-1], refs[-1]
    rows = sums[0].shape[1]
    for i, ref in enumerate(sums):
        basis[i * rows : (i + 1) * rows, :] = ref[0]
    toks = tokens.shape[0] // MOST
    for k in range(MOST):

        @pl.when(pl.program_id(0) == k)
        def _():
            for i in range(MOST):
                strip = slice(i * toks, (i + 1) * toks)
                outs[k][strip, :] = mul(tokens[strip, LANES:], basis[...]).astype(BF16)


def project(tokens, sums):
    rank = sums[0].shape[-1]
    total, width = tokens.shape
    depth = width - LANES
    return pl.pallas_call(
        functools.partial(project_kernel, len(sums)),
        grid=(MOST,),
        in_specs=[pl.BlockSpec((total, width), lambda k: (0, 0))]
        + [pl.BlockSpec((1,) + value.shape[1:], lambda k: (k, 0, 0)) for value in sums],
        out_specs=[pl.BlockSpec((total, rank), lambda k: (0, 0))] * MOST,
        out_shape=[jax.ShapeDtypeStruct((total, rank), BF16)] * MOST,
        scratch_shapes=[pltpu.VMEM((depth, rank), BF16)],
        compiler_params=params(),
        cost_estimate=cost(2 * MOST * total * depth * rank, 4 * MOST * total * rank),
        name="project",
    )(tokens, *sums)


def reciprocal(value):
    guess = pl.reciprocal(value, approx=True)
    guess = guess * (2.0 - value * guess)
    return guess * (2.0 - value * guess)


def factor_kernel(tile, gram_ref, inverse_ref, work_ref):
    rank = gram_ref.shape[0]
    steps = rank // tile
    row_of = lax.broadcasted_iota(jnp.int32, (tile, tile), 0)
    col_of = lax.broadcasted_iota(jnp.int32, (tile, tile), 1)
    corners = [
        jnp.where(row_of == col_of, gram_ref[t * tile : (t + 1) * tile, t * tile : (t + 1) * tile], 0.0)
        for t in range(steps)
    ]
    scale = lax.rsqrt(
        jnp.concatenate([jnp.sum(c, axis=0, keepdims=True) for c in corners], axis=1)
    )
    for t in range(steps):
        strip = slice(t * tile, (t + 1) * tile)
        scale_rows = lax.rsqrt(jnp.sum(corners[t], axis=1, keepdims=True))
        work_ref[strip, :] = gram_ref[strip, :] * scale_rows * scale
    lane = lax.broadcasted_iota(jnp.int32, (8, tile), 1)
    sub = lax.broadcasted_iota(jnp.int32, (8, tile), 0)
    lane_row = lane[:1]

    def step(index, carry):
        base = pl.multiple_of(index * tile, tile)
        here = pl.ds(base, tile)
        strips = [
            work_ref[pl.ds(pl.multiple_of(base + 8 * s, 8), 8), here] for s in range(tile // 8)
        ]
        for j in range(0, tile, 2):
            first, inner = divmod(j, 8)
            both = strips[first]
            row0, row1 = both[inner : inner + 1, :], both[inner + 1 : inner + 2, :]
            columns = [
                [jnp.broadcast_to(strip[:, i : i + 1], strip.shape) for i in (j, j + 1)]
                for strip in strips[first:]
            ]
            column0, column1 = columns[0]
            a, b = column0[inner : inner + 1, :], column0[inner + 1 : inner + 2, :]
            d = column1[inner + 1 : inner + 2, :]
            inverse_a = reciprocal(a)
            inverse_d = a * reciprocal(a * d - b * b)
            ratio = b * inverse_a
            later = jnp.where(lane_row == j, 0.0, row1) - ratio * jnp.where(lane_row == j, 1.0, row0)
            scaled0 = jnp.where(lane_row == j, 1.0, jnp.where(lane_row == j + 1, 0.0, row0)) * inverse_a
            scaled1 = jnp.where(lane_row == j + 1, 1.0, later) * inverse_d
            for s in range(first, tile // 8):
                strip = strips[s]
                column0, column1 = columns[s - first]
                column1 = column1 - column0 * ratio
                new = jnp.where((lane == j) | (lane == j + 1), 0.0, strip)
                new = new - column0 * scaled0 - column1 * scaled1
                if s == first:
                    new = jnp.where(sub > inner + 1, new, jnp.where(sub == inner + 1, later, strip))
                strips[s] = new
        block = jnp.concatenate(strips, axis=0)
        pivots = jnp.sum(jnp.where(row_of == col_of, block, 0.0), axis=1, keepdims=True)
        unit = jnp.where(row_of == col_of, 1.0, 0.0)
        own = jnp.where(col_of < row_of, block, unit) / jnp.sqrt(pivots)
        work_ref[here, here] = unit
        right = exact(own, work_ref[here, :], ((1,), (0,)))
        columns = lax.broadcasted_iota(jnp.int32, (tile, rank), 1)
        inverse_ref[here, :] = jnp.where(columns < base + tile, right * scale, 0.0)
        for s in range(steps - 1):

            @pl.when(index == s)
            def _():
                below = slice((s + 1) * tile, rank)
                mine = slice(s * tile, (s + 1) * tile)
                left = exact(work_ref[below, mine], own, ((1,), (1,)))
                work_ref[below, mine] = jnp.zeros((rank - (s + 1) * tile, tile), F32)
                work_ref[below, :] = work_ref[below, :] - exact(left, right, ((1,), (0,)))

        return carry

    lax.fori_loop(0, steps, step, 0)


def factored(gram):
    rank = gram.shape[0]
    return pl.pallas_call(
        functools.partial(factor_kernel, min(LANES, rank)),
        out_shape=jax.ShapeDtypeStruct((rank, rank), F32),
        in_specs=[whole()],
        out_specs=whole(),
        scratch_shapes=[pltpu.VMEM((rank, rank), F32)],
        compiler_params=params(),
        cost_estimate=cost(4e10, 8 * rank * rank),
        name="factored",
    )(gram)


def coefficient_kernel(inverse, raw, out):
    out[0] = mul3(inverse[...], raw[0], ((1,), (0,))).astype(BF16)


def coefficients(inverse, raw):
    sides, rank, hid = raw.shape
    side = pl.BlockSpec((1, rank, hid), lambda i: (i, 0, 0))
    return pl.pallas_call(
        coefficient_kernel,
        grid=(sides,),
        in_specs=[pl.BlockSpec((rank, rank), lambda i: (0, 0)), side],
        out_specs=side,
        out_shape=jax.ShapeDtypeStruct(raw.shape, BF16),
        compiler_params=params(),
        cost_estimate=cost(6 * sides * rank * rank * hid, 6 * sides * rank * hid),
        name="coefficients",
    )(inverse, raw)


def hidden_kernel(toks, groups, meta, inverse, mine, others, tokens, *refs):
    arrived, outs = refs[:MOST], refs[MOST:]
    group = meta[2 * MOST] // MOST
    lane = lax.broadcasted_iota(jnp.int32, tokens.shape, 1)
    picked = (lane == group) | (lane == group + groups)
    share = jnp.sum(jnp.where(picked, tokens[...].astype(F32), 0.0), axis=1, keepdims=True)
    raw = []
    for k in range(MOST):
        total = jnp.zeros((toks, inverse.shape[0]), F32)
        for mask in range(MOST):
            source = (k ^ mask) * toks
            total += arrived[mask][source : source + toks, :].astype(F32)
        raw.append(total)
    projected = mul3(jnp.concatenate(raw, axis=0), inverse[...], ((1,), (1,))).astype(BF16)
    hid = mine.shape[2]
    for d, side in enumerate((mine, others)):
        gate = mul(projected, side[0])
        hidden = gate / (1.0 + jnp.exp(-gate)) * mul(projected, side[1]) * share
        hidden = hidden.astype(BF16)
        block = pl.ds(pl.multiple_of(meta[d * MOST] // MOST * hid, LANES), hid)
        for k in range(MOST):
            x, y = k % 2, k // 2
            rows = hidden[k * toks : (k + 1) * toks]
            outs[x][0, y * toks : (y + 1) * toks, block] = rows
            outs[2 + y][0, x * toks : (x + 1) * toks, block] = rows
        outs[4][0, :, block] = hidden


def hidden_rows(meta, inverse, coeff, other_coeff, tokens, arrived, toks):
    rank, hid = coeff.shape[1:]
    groups = tokens.shape[0] // (MOST * toks)
    block = MOST * toks
    out = jax.ShapeDtypeStruct((groups, block // 2, 2 * hid), BF16)
    coeff_spec = pl.BlockSpec((2, rank, hid), lambda g: (0, 0, 0))
    return pl.pallas_call(
        functools.partial(hidden_kernel, toks, groups),
        grid=(groups,),
        in_specs=[
            scalars(),
            pl.BlockSpec((rank, rank), lambda g: (0, 0)),
            coeff_spec,
            coeff_spec,
            pl.BlockSpec((block, LANES), lambda g: (g, 0)),
        ]
        + [pl.BlockSpec((block, rank), lambda g: (g, 0))] * MOST,
        out_specs=[pl.BlockSpec((1, block // 2, 2 * hid), lambda g: (g, 0, 0))] * 4
        + [pl.BlockSpec((1, block, 2 * hid), lambda g: (g, 0, 0))],
        out_shape=[out] * 4 + [jax.ShapeDtypeStruct((groups, block, 2 * hid), BF16)],
        compiler_params=params(),
        cost_estimate=cost(groups * block * rank * (6 * rank + 8 * hid), 16 * groups * block * hid),
        name="hidden_rows",
    )(meta, inverse, coeff, other_coeff, tokens, *arrived)


def group_masks(experts):
    masks, mask = [], MOST
    while mask < experts:
        masks.insert(0, mask)
        mask *= 2
    return masks


def column_chunks(depth, bits):
    near = list(range(bits - 1, 1, -1))
    orders = [[0, 1] + near, [1, 0] + near, near + [0, 1]]
    units = depth // LANES
    if units % 56:
        return [(0, depth, orders[0])]
    sizes = [(11, 0), (11, 1), (12, 2), (11, 0), (11, 1)]
    chunks, start = [], 0
    for size, order in sizes:
        width = size * (units // 56) * LANES
        chunks.append((start, width, orders[order]))
        start += width
    return chunks


def scattered_answers(sides, down, toks):
    experts = lax.axis_size("expert")
    masks = [1, 2] + group_masks(experts)
    bits = len(masks)
    chunks = column_chunks(down.shape[1], bits)
    groups = experts // MOST
    halves = {0: sides[0:2], 1: sides[2:4]}
    if groups > 1:
        halves[bits - 1] = (sides[4][: groups // 2], sides[4][groups // 2 :])

    def answered(rows, start, width):
        return mul(rows.reshape(-1, rows.shape[-1]), down[:, start : start + width])

    first = [
        swap_expert(answered(halves[order[0]][1], start, width).astype(BF16), masks[order[0]])
        for start, width, order in chunks
    ]
    def added(i):
        start, width, order = chunks[i]
        return (answered(halves[order[0]][0], start, width) + first[i].astype(F32)).astype(BF16)

    values = [None] * len(chunks)
    if len(chunks) > 2:
        values[2] = added(2)
        _, first[0], first[1] = lax.optimization_barrier((values[2], first[0], first[1]))
    values = [added(i) if value is None else value for i, value in enumerate(values)]
    left = [[bit for bit in range(bits - 1, -1, -1) if bit != order[0]] for _, _, order in chunks]
    for step in range(1, bits):
        for i, (_, width, order) in enumerate(chunks):
            bit = order[step]
            axis = left[i].index(bit)
            value = values[i].reshape((2,) * len(left[i]) + (toks, width))
            kept, out = (lax.index_in_dim(value, side, axis, keepdims=False) for side in (0, 1))
            values[i] = (kept.astype(F32) + swap_expert(out, masks[bit]).astype(F32)).astype(BF16)
            left[i].remove(bit)
    return jnp.concatenate([value.reshape(toks, -1) for value in values], axis=1)


def on_device(tokens, gate_weight, up_weight, down_weight, sketch, clusters, routes, route_weights):
    experts = lax.axis_size("expert")
    position = lax.axis_index("expert").astype(jnp.int32)
    place = position % MOST
    groups = experts // MOST
    half = lax.axis_index("dp").astype(jnp.int32)
    gate_rows = gate_weight[0]
    up_rows = up_weight[0]
    depth, rank = gate_rows.shape[0], sketch.shape[-1]
    rows = depth // 2 // MOST
    toks = tokens.shape[0]
    steps = jnp.arange(2 * MOST, dtype=jnp.int32)
    order = ((steps // MOST) ^ half) * MOST + ((steps % MOST) ^ place)
    meta = jnp.concatenate([order, position[None], clusters])

    down_rows = lax.all_gather(down_weight[0], "dp", axis=0, tiled=True)

    sent_half = swap_dp(sketch_half(meta, gate_rows, up_rows, sketch[0], 1, rows))
    own_half = sketch_half(meta, gate_rows, up_rows, sketch[0], 0, rows)
    pieces = token_pieces(meta, tokens, routes, route_weights, groups, rows, place)
    plane = [pieces[0]] + [swap_expert(pieces[k], k) for k in range(1, MOST)]
    spread = jnp.concatenate(plane, axis=0)
    spread, own_half = lax.optimization_barrier((spread, own_half))

    chunks = 2 if rows % 32 == 0 else 1
    chunk = rows // chunks
    own = [(own_half[k].astype(F32) + sent_half[k].astype(F32)).astype(BF16) for k in range(MOST)]
    got = [own[0]] + [swap_expert(own[k], k) for k in range(1, MOST)]
    masks = group_masks(experts)
    for mask in masks[:-1]:
        spread = jnp.concatenate([spread, swap_expert(spread, mask)], axis=0)
    spread, got = lax.optimization_barrier((spread, got))
    sums, *sends = group_sums(meta, got, chunks)
    other_sums = swap_dp(sums)
    back = []
    for c in range(chunks):
        first = c * (MOST - 1)
        back.append(
            [sums[0, c * chunk : (c + 1) * chunk]]
            + [swap_expert(sends[first + k - 1], k) for k in range(1, MOST)]
        )
    if masks:
        spread, sums = lax.optimization_barrier((spread, sums))
        spread = jnp.concatenate([spread, swap_expert(spread, masks[-1])], axis=0)
    other_sums, back[0] = lax.optimization_barrier((other_sums, back[0]))
    before = ()
    for c in range(chunks):
        if c == chunks - 1:
            before, back[c] = lax.optimization_barrier((before, back[c]))
        mine = stacked(back[c])
        if c == chunks - 1:
            mine, spread = lax.optimization_barrier((mine, spread))
        other = swap_dp(mine)
        if c == chunks - 1:
            parts = project(spread, [sums, other_sums])
            parts, gate_rows, other = lax.optimization_barrier((parts, gate_rows, other))
        before = crossed(meta, mine, other, gate_rows, up_rows, c, chunks, before)
    gram, raw = before
    if lax.axis_size("tensor") > 1:
        gram, raw = lax.psum((gram, raw), "tensor")
        parts = [lax.psum(value.astype(F32), "tensor").astype(BF16) for value in parts]
    arrived = [parts[0]] + [swap_expert(parts[k], k) for k in range(1, MOST)]
    inverse = factored(gram)
    inverse, arrived = lax.optimization_barrier((inverse, arrived))
    coeff = coefficients(inverse, raw)
    other_coeff = swap_dp(coeff)
    shares = spread[:, :LANES]
    sides = hidden_rows(meta, inverse, coeff, other_coeff, shares, arrived, toks)
    return scattered_answers(sides, down_rows, toks)


def solution(mesh):
    return jax.shard_map(
        on_device,
        mesh=mesh,
        in_specs=(
            P(("expert", "dp"), "tensor"),
            P("expert", "tensor", "dp"),
            P("expert", "tensor", "dp"),
            P("expert", "dp", "tensor"),
            P("expert", None, "dp", None),
            P(),
            P(("expert", "dp"), None),
            P(("expert", "dp"), None),
        ),
        out_specs=P(("expert", "dp"), "tensor"),
        check_vma=False,
    )
```

```python
import functools

import jax
import jax.numpy as jnp
from jax import lax
from jax.experimental import pallas as pl
from jax.experimental.pallas import tpu as pltpu
from jax.sharding import PartitionSpec as P

MOST = 4
LANES = 128
VMEM_BYTES = 56 * 1024 * 1024

HIGHEST = lax.Precision.HIGHEST
F32 = jnp.float32
BF16 = jnp.bfloat16


def swap_expert(value, mask):
    count = lax.axis_size("expert")
    return lax.ppermute(value, "expert", [(source, source ^ mask) for source in range(count)])


def swap_dp(value):
    count = lax.axis_size("dp")
    return lax.ppermute(value, "dp", [(source, count - 1 - source) for source in range(count)])


def shift_groups(value, steps):
    count = lax.axis_size("expert")
    moves = [(s, s + steps) for s in range(count) if 0 <= s + steps < count]
    return lax.ppermute(value, "expert", moves)


def whole():
    return pl.BlockSpec(memory_space=pltpu.VMEM)


def scalars():
    return pl.BlockSpec(memory_space=pltpu.SMEM)


def params(**more):
    return pltpu.CompilerParams(vmem_limit_bytes=VMEM_BYTES, **more)


def cost(flops, moved):
    return pl.CostEstimate(flops=int(flops), bytes_accessed=int(moved), transcendentals=0)


def mul(a, b, dims=((1,), (0,))):
    return lax.dot_general(a, b, (dims, ((), ())), preferred_element_type=F32)


def exact(a, b, dims):
    return lax.dot_general(a, b, (dims, ((), ())), precision=HIGHEST, preferred_element_type=F32)


def parts_of(value):
    high = value.astype(BF16)
    return high, (value - high.astype(F32)).astype(BF16)


def mul3(a, b, dims):
    (a0, a1), (b0, b1) = parts_of(a), parts_of(b)
    return mul(a0, b0, dims) + (mul(a0, b1, dims) + mul(a1, b0, dims))


def token_kernel(groups, rows, meta, tokens, routes, weights, *pieces):
    place = lax.rem(meta[2 * MOST], MOST)
    toks = tokens.shape[0]
    lane = lax.broadcasted_iota(jnp.int32, (toks, LANES), 1)
    group = lax.rem(lane, groups)
    for k in range(MOST):
        expert = group * MOST + (place ^ k)
        share = jnp.zeros((toks, LANES), F32)
        for t in range(routes.shape[1]):
            share += jnp.where(routes[:, t : t + 1] == expert, weights[:, t : t + 1], 0.0)
        high, low = parts_of(share)
        pieces[k][:, :LANES] = jnp.where(
            lane < groups, high.astype(F32), low.astype(F32)
        ).astype(BF16)
        for d in range(2):
            start = pl.multiple_of(meta[d * MOST + k] * rows, LANES)
            pieces[k][:, LANES + d * rows : LANES + (d + 1) * rows] = tokens[:, pl.ds(start, rows)]


def token_pieces(meta, tokens, routes, weights, groups, rows, place):
    toks = tokens.shape[0]
    if rows % LANES == 0:
        return pl.pallas_call(
            functools.partial(token_kernel, groups, rows),
            out_shape=[jax.ShapeDtypeStruct((toks, LANES + 2 * rows), BF16)] * MOST,
            in_specs=[scalars(), whole(), whole(), whole()],
            out_specs=[whole()] * MOST,
            compiler_params=params(),
            name="token_pieces",
        )(meta, tokens, routes, weights)
    lane = jnp.arange(LANES, dtype=jnp.int32)
    pieces = []
    for k in range(MOST):
        expert = (lane % groups) * MOST + (place ^ k)
        share = jnp.sum(jnp.where(routes[:, :, None] == expert, weights[:, :, None], 0.0), axis=1)
        high, low = parts_of(share)
        columns = [
            lax.dynamic_slice_in_dim(tokens, meta[d * MOST + k] * rows, rows, axis=1)
            for d in range(2)
        ]
        pieces.append(jnp.concatenate([jnp.where(lane < groups, high, low)] + columns, axis=1))
    return pieces


def sketch_kernel(meta, gate, up, sketch, out):
    both = jnp.concatenate([gate[...], up[...]], axis=1)
    out[0] = mul(both, jnp.concatenate([sketch[0], sketch[1]], axis=0)).astype(BF16)


def sketch_half(meta, gate, up, sketch, side, rows):
    hid, rank = sketch.shape[1:]
    row_block = pl.BlockSpec((rows, hid), lambda k, meta: (meta[side * MOST + k], 0))
    return pl.pallas_call(
        sketch_kernel,
        grid_spec=pltpu.PrefetchScalarGridSpec(
            num_scalar_prefetch=1,
            grid=(MOST,),
            in_specs=[row_block, row_block, pl.BlockSpec((2, hid, rank), lambda k, meta: (0, 0, 0))],
            out_specs=pl.BlockSpec((1, rows, rank), lambda k, meta: (k, 0, 0)),
        ),
        out_shape=jax.ShapeDtypeStruct((MOST, rows, rank), BF16),
        compiler_params=params(),
        cost_estimate=cost(4 * MOST * rows * hid * rank, 4 * MOST * rows * hid),
        name="sketch_half",
    )(meta, gate, up, sketch)


def chosen(values, names, name):
    total = jnp.zeros(values[0].shape, F32)
    for value, own in zip(values, names):
        total += jnp.where(own == name, value, 0.0)
    return total


def ends_kernel(meta, *refs):
    values = [ref[...].astype(F32) for ref in refs[:MOST]]
    tail, head = refs[MOST:]
    position = meta[2 * MOST]
    place = lax.rem(position, MOST)
    first = position - place
    base = 2 * MOST + 1
    names = [meta[base + first + (place ^ k)] for k in range(MOST)]
    tail[...] = chosen(values, names, meta[base + first + MOST - 1]).astype(BF16)
    head[...] = chosen(values, names, meta[base + first]).astype(BF16)


def totals_kernel(experts, chunks, meta, *refs):
    values = [ref[...].astype(F32) for ref in refs[:MOST]]
    below, above = (ref[...].astype(F32) for ref in refs[MOST : MOST + 2])
    stacked, sends = refs[MOST + 2], refs[MOST + 3 :]
    position = meta[2 * MOST]
    place = lax.rem(position, MOST)
    first = position - place
    base = 2 * MOST + 1
    names = [meta[base + first + (place ^ k)] for k in range(MOST)]
    below_name = jnp.where(first > 0, meta[base + jnp.maximum(first - 1, 0)], -1)
    above_name = jnp.where(
        first + MOST < experts, meta[base + jnp.minimum(first + MOST, experts - 1)], -1
    )
    for k in range(MOST):
        total = chosen(values, names, names[k])
        total += jnp.where(names[k] == below_name, below, 0.0)
        total += jnp.where(names[k] == above_name, above, 0.0)
        total = total.astype(BF16)
        stacked[k] = total
        if k:
            for c in range(chunks):
                part = sends[c * (MOST - 1) + k - 1]
                rows = part.shape[0]
                part[...] = total[c * rows : (c + 1) * rows]


def stack_kernel(*refs):
    for k in range(MOST):
        refs[MOST][k] = refs[k][...]


def group_sums(meta, got, chunks):
    shape = got[0].shape
    experts = lax.axis_size("expert")
    piece = jax.ShapeDtypeStruct(shape, BF16)
    part = jax.ShapeDtypeStruct((shape[0] // chunks, shape[1]), BF16)
    tail, head = pl.pallas_call(
        ends_kernel,
        out_shape=[piece, piece],
        in_specs=[scalars()] + [whole()] * MOST,
        out_specs=[whole()] * 2,
        compiler_params=params(),
        name="end_sums",
    )(meta, *got)
    below = shift_groups(tail, MOST)
    above = shift_groups(head, -MOST)
    return pl.pallas_call(
        functools.partial(totals_kernel, experts, chunks),
        out_shape=[jax.ShapeDtypeStruct((MOST,) + shape, BF16)] + [part] * (chunks * (MOST - 1)),
        in_specs=[scalars()] + [whole()] * (MOST + 2),
        out_specs=[whole()] * (1 + chunks * (MOST - 1)),
        compiler_params=params(),
        name="cluster_sums",
    )(meta, *got, below, above)


def stacked(values):
    return pl.pallas_call(
        stack_kernel,
        out_shape=jax.ShapeDtypeStruct((MOST,) + values[0].shape, BF16),
        in_specs=[whole()] * MOST,
        out_specs=whole(),
        compiler_params=params(),
        name="own_sums",
    )(*values)


def cross_kernel(started, meta, own, other, gate, gate_other, up, up_other, *refs):
    if started:
        old_gram, old_raw, gram, raw = refs
    else:
        gram, raw = refs
    step = pl.program_id(0)

    @pl.when(step == 0)
    def _():
        gram[...] = old_gram[...] if started else jnp.zeros(gram.shape, F32)
        raw[...] = old_raw[...] if started else jnp.zeros(raw.shape, F32)

    rows = jnp.concatenate([own[0], other[0]], axis=0)
    turned = rows.T
    gram[...] += mul(turned, rows)
    raw[0] += mul(turned, jnp.concatenate([gate[...], gate_other[...]], axis=0))
    raw[1] += mul(turned, jnp.concatenate([up[...], up_other[...]], axis=0))


def crossed(meta, own, other, gate, up, chunk, chunks, before):
    _, rows, rank = own.shape
    hid = gate.shape[1]
    sum_block = pl.BlockSpec((1, rows, rank), lambda i, meta: (i, 0, 0))
    row_block = pl.BlockSpec((rows, hid), lambda i, meta: (meta[i] * chunks + chunk, 0))
    other_block = pl.BlockSpec((rows, hid), lambda i, meta: (meta[MOST + i] * chunks + chunk, 0))
    gram_spec = pl.BlockSpec((rank, rank), lambda i, meta: (0, 0))
    raw_spec = pl.BlockSpec((2, rank, hid), lambda i, meta: (0, 0, 0))
    return pl.pallas_call(
        functools.partial(cross_kernel, bool(before)),
        grid_spec=pltpu.PrefetchScalarGridSpec(
            num_scalar_prefetch=1,
            grid=(MOST,),
            in_specs=[sum_block, sum_block, row_block, other_block, row_block, other_block]
            + ([gram_spec, raw_spec] if before else []),
            out_specs=[gram_spec, raw_spec],
        ),
        out_shape=[
            jax.ShapeDtypeStruct((rank, rank), F32),
            jax.ShapeDtypeStruct((2, rank, hid), F32),
        ],
        compiler_params=params(),
        cost_estimate=cost(4 * MOST * rows * rank * (rank + 2 * hid), 8 * MOST * rows * rank * 3),
        name="crossed",
    )(meta, own, other, gate, gate, up, up, *before)


def project_kernel(count, tokens, *refs):
    sums, outs, basis = refs[:count], refs[count:-1], refs[-1]
    rows = sums[0].shape[1]
    for i, ref in enumerate(sums):
        basis[i * rows : (i + 1) * rows, :] = ref[0]
    toks = tokens.shape[0] // MOST
    for k in range(MOST):

        @pl.when(pl.program_id(0) == k)
        def _():
            for i in range(MOST):
                strip = slice(i * toks, (i + 1) * toks)
                outs[k][strip, :] = mul(tokens[strip, LANES:], basis[...]).astype(BF16)


def project(tokens, sums):
    rank = sums[0].shape[-1]
    total, width = tokens.shape
    depth = width - LANES
    return pl.pallas_call(
        functools.partial(project_kernel, len(sums)),
        grid=(MOST,),
        in_specs=[pl.BlockSpec((total, width), lambda k: (0, 0))]
        + [pl.BlockSpec((1,) + value.shape[1:], lambda k: (k, 0, 0)) for value in sums],
        out_specs=[pl.BlockSpec((total, rank), lambda k: (0, 0))] * MOST,
        out_shape=[jax.ShapeDtypeStruct((total, rank), BF16)] * MOST,
        scratch_shapes=[pltpu.VMEM((depth, rank), BF16)],
        compiler_params=params(),
        cost_estimate=cost(2 * MOST * total * depth * rank, 4 * MOST * total * rank),
        name="project",
    )(tokens, *sums)


def reciprocal(value):
    guess = pl.reciprocal(value, approx=True)
    guess = guess * (2.0 - value * guess)
    return guess * (2.0 - value * guess)


def factor_kernel(tile, gram_ref, inverse_ref, work_ref):
    rank = gram_ref.shape[0]
    steps = rank // tile
    row_of = lax.broadcasted_iota(jnp.int32, (tile, tile), 0)
    col_of = lax.broadcasted_iota(jnp.int32, (tile, tile), 1)
    corners = [
        jnp.where(row_of == col_of, gram_ref[t * tile : (t + 1) * tile, t * tile : (t + 1) * tile], 0.0)
        for t in range(steps)
    ]
    scale = lax.rsqrt(
        jnp.concatenate([jnp.sum(c, axis=0, keepdims=True) for c in corners], axis=1)
    )
    for t in range(steps):
        strip = slice(t * tile, (t + 1) * tile)
        scale_rows = lax.rsqrt(jnp.sum(corners[t], axis=1, keepdims=True))
        work_ref[strip, :] = gram_ref[strip, :] * scale_rows * scale
    lane = lax.broadcasted_iota(jnp.int32, (8, tile), 1)
    sub = lax.broadcasted_iota(jnp.int32, (8, tile), 0)
    lane_row = lane[:1]

    def step(index, carry):
        base = pl.multiple_of(index * tile, tile)
        here = pl.ds(base, tile)
        strips = [
            work_ref[pl.ds(pl.multiple_of(base + 8 * s, 8), 8), here] for s in range(tile // 8)
        ]
        for j in range(0, tile, 2):
            first, inner = divmod(j, 8)
            both = strips[first]
            row0, row1 = both[inner : inner + 1, :], both[inner + 1 : inner + 2, :]
            columns = [
                [jnp.broadcast_to(strip[:, i : i + 1], strip.shape) for i in (j, j + 1)]
                for strip in strips[first:]
            ]
            column0, column1 = columns[0]
            a, b = column0[inner : inner + 1, :], column0[inner + 1 : inner + 2, :]
            d = column1[inner + 1 : inner + 2, :]
            inverse_a = reciprocal(a)
            inverse_d = a * reciprocal(a * d - b * b)
            ratio = b * inverse_a
            later = jnp.where(lane_row == j, 0.0, row1) - ratio * jnp.where(lane_row == j, 1.0, row0)
            scaled0 = jnp.where(lane_row == j, 1.0, jnp.where(lane_row == j + 1, 0.0, row0)) * inverse_a
            scaled1 = jnp.where(lane_row == j + 1, 1.0, later) * inverse_d
            for s in range(first, tile // 8):
                strip = strips[s]
                column0, column1 = columns[s - first]
                column1 = column1 - column0 * ratio
                new = jnp.where((lane == j) | (lane == j + 1), 0.0, strip)
                new = new - column0 * scaled0 - column1 * scaled1
                if s == first:
                    new = jnp.where(sub > inner + 1, new, jnp.where(sub == inner + 1, later, strip))
                strips[s] = new
        block = jnp.concatenate(strips, axis=0)
        pivots = jnp.sum(jnp.where(row_of == col_of, block, 0.0), axis=1, keepdims=True)
        unit = jnp.where(row_of == col_of, 1.0, 0.0)
        own = jnp.where(col_of < row_of, block, unit) / jnp.sqrt(pivots)
        work_ref[here, here] = unit
        right = exact(own, work_ref[here, :], ((1,), (0,)))
        columns = lax.broadcasted_iota(jnp.int32, (tile, rank), 1)
        inverse_ref[here, :] = jnp.where(columns < base + tile, right * scale, 0.0)
        for s in range(steps - 1):

            @pl.when(index == s)
            def _():
                below = slice((s + 1) * tile, rank)
                mine = slice(s * tile, (s + 1) * tile)
                left = exact(work_ref[below, mine], own, ((1,), (1,)))
                work_ref[below, mine] = jnp.zeros((rank - (s + 1) * tile, tile), F32)
                work_ref[below, :] = work_ref[below, :] - exact(left, right, ((1,), (0,)))

        return carry

    lax.fori_loop(0, steps, step, 0)


def factored(gram):
    rank = gram.shape[0]
    return pl.pallas_call(
        functools.partial(factor_kernel, min(LANES, rank)),
        out_shape=jax.ShapeDtypeStruct((rank, rank), F32),
        in_specs=[whole()],
        out_specs=whole(),
        scratch_shapes=[pltpu.VMEM((rank, rank), F32)],
        compiler_params=params(),
        cost_estimate=cost(4e10, 8 * rank * rank),
        name="factored",
    )(gram)


def coefficient_kernel(inverse, raw, out):
    out[0] = mul3(inverse[...], raw[0], ((1,), (0,))).astype(BF16)


def coefficients(inverse, raw):
    sides, rank, hid = raw.shape
    side = pl.BlockSpec((1, rank, hid), lambda i: (i, 0, 0))
    return pl.pallas_call(
        coefficient_kernel,
        grid=(sides,),
        in_specs=[pl.BlockSpec((rank, rank), lambda i: (0, 0)), side],
        out_specs=side,
        out_shape=jax.ShapeDtypeStruct(raw.shape, BF16),
        compiler_params=params(),
        cost_estimate=cost(6 * sides * rank * rank * hid, 6 * sides * rank * hid),
        name="coefficients",
    )(inverse, raw)


def hidden_kernel(toks, groups, meta, inverse, mine, others, tokens, *refs):
    arrived, outs = refs[:MOST], refs[MOST:]
    group = meta[2 * MOST] // MOST
    lane = lax.broadcasted_iota(jnp.int32, tokens.shape, 1)
    picked = (lane == group) | (lane == group + groups)
    share = jnp.sum(jnp.where(picked, tokens[...].astype(F32), 0.0), axis=1, keepdims=True)
    raw = []
    for k in range(MOST):
        total = jnp.zeros((toks, inverse.shape[0]), F32)
        for mask in range(MOST):
            source = (k ^ mask) * toks
            total += arrived[mask][source : source + toks, :].astype(F32)
        raw.append(total)
    projected = mul3(jnp.concatenate(raw, axis=0), inverse[...], ((1,), (1,))).astype(BF16)
    hid = mine.shape[2]
    for d, side in enumerate((mine, others)):
        gate = mul(projected, side[0])
        hidden = gate / (1.0 + jnp.exp(-gate)) * mul(projected, side[1]) * share
        hidden = hidden.astype(BF16)
        block = pl.ds(pl.multiple_of(meta[d * MOST] // MOST * hid, LANES), hid)
        for k in range(MOST):
            x, y = k % 2, k // 2
            rows = hidden[k * toks : (k + 1) * toks]
            outs[x][0, y * toks : (y + 1) * toks, block] = rows
            outs[2 + y][0, x * toks : (x + 1) * toks, block] = rows
        outs[4][0, :, block] = hidden


def hidden_rows(meta, inverse, coeff, other_coeff, tokens, arrived, toks):
    rank, hid = coeff.shape[1:]
    groups = tokens.shape[0] // (MOST * toks)
    block = MOST * toks
    out = jax.ShapeDtypeStruct((groups, block // 2, 2 * hid), BF16)
    coeff_spec = pl.BlockSpec((2, rank, hid), lambda g: (0, 0, 0))
    return pl.pallas_call(
        functools.partial(hidden_kernel, toks, groups),
        grid=(groups,),
        in_specs=[
            scalars(),
            pl.BlockSpec((rank, rank), lambda g: (0, 0)),
            coeff_spec,
            coeff_spec,
            pl.BlockSpec((block, LANES), lambda g: (g, 0)),
        ]
        + [pl.BlockSpec((block, rank), lambda g: (g, 0))] * MOST,
        out_specs=[pl.BlockSpec((1, block // 2, 2 * hid), lambda g: (g, 0, 0))] * 4
        + [pl.BlockSpec((1, block, 2 * hid), lambda g: (g, 0, 0))],
        out_shape=[out] * 4 + [jax.ShapeDtypeStruct((groups, block, 2 * hid), BF16)],
        compiler_params=params(),
        cost_estimate=cost(groups * block * rank * (6 * rank + 8 * hid), 16 * groups * block * hid),
        name="hidden_rows",
    )(meta, inverse, coeff, other_coeff, tokens, *arrived)


def group_masks(experts):
    masks, mask = [], MOST
    while mask < experts:
        masks.insert(0, mask)
        mask *= 2
    return masks


def column_chunks(depth, bits):
    near = list(range(bits - 1, 1, -1))
    orders = [[0, 1] + near, [1, 0] + near, near + [0, 1]]
    units = depth // LANES
    if units % 56:
        return [(0, depth, orders[0])]
    sizes = [(8, 0), (8, 1)] * 3 + [(8, 2)]
    chunks, start = [], 0
    for size, order in sizes:
        width = size * (units // 56) * LANES
        chunks.append((start, width, orders[order]))
        start += width
    return chunks


def scattered_answers(sides, down, toks):
    experts = lax.axis_size("expert")
    masks = [1, 2] + group_masks(experts)
    bits = len(masks)
    chunks = column_chunks(down.shape[1], bits)
    groups = experts // MOST
    halves = {0: sides[0:2], 1: sides[2:4]}
    if groups > 1:
        halves[bits - 1] = (sides[4][: groups // 2], sides[4][groups // 2 :])

    def answered(rows, start, width):
        return mul(rows.reshape(-1, rows.shape[-1]), down[:, start : start + width])

    first = [
        swap_expert(answered(halves[order[0]][1], start, width).astype(BF16), masks[order[0]])
        for start, width, order in chunks
    ]
    def added(i):
        start, width, order = chunks[i]
        return (answered(halves[order[0]][0], start, width) + first[i].astype(F32)).astype(BF16)

    values = [None] * len(chunks)
    if len(chunks) > 4:
        values[-1] = added(len(chunks) - 1)
        _, first[:4] = lax.optimization_barrier((values[-1], first[:4]))
    values = [added(i) if value is None else value for i, value in enumerate(values)]
    left = [[bit for bit in range(bits - 1, -1, -1) if bit != order[0]] for _, _, order in chunks]
    for step in range(1, bits):
        for i, (_, width, order) in enumerate(chunks):
            bit = order[step]
            axis = left[i].index(bit)
            value = values[i].reshape((2,) * len(left[i]) + (toks, width))
            kept, out = (lax.index_in_dim(value, side, axis, keepdims=False) for side in (0, 1))
            values[i] = (kept.astype(F32) + swap_expert(out, masks[bit]).astype(F32)).astype(BF16)
            left[i].remove(bit)
    return jnp.concatenate([value.reshape(toks, -1) for value in values], axis=1)


def on_device(tokens, gate_weight, up_weight, down_weight, sketch, clusters, routes, route_weights):
    experts = lax.axis_size("expert")
    position = lax.axis_index("expert").astype(jnp.int32)
    place = position % MOST
    groups = experts // MOST
    half = lax.axis_index("dp").astype(jnp.int32)
    gate_rows = gate_weight[0]
    up_rows = up_weight[0]
    depth, rank = gate_rows.shape[0], sketch.shape[-1]
    rows = depth // 2 // MOST
    toks = tokens.shape[0]
    steps = jnp.arange(2 * MOST, dtype=jnp.int32)
    order = ((steps // MOST) ^ half) * MOST + ((steps % MOST) ^ place)
    meta = jnp.concatenate([order, position[None], clusters])

    down_rows = lax.all_gather(down_weight[0], "dp", axis=0, tiled=True)

    sent_half = swap_dp(sketch_half(meta, gate_rows, up_rows, sketch[0], 1, rows))
    own_half = sketch_half(meta, gate_rows, up_rows, sketch[0], 0, rows)
    pieces = token_pieces(meta, tokens, routes, route_weights, groups, rows, place)
    plane = [pieces[0]] + [swap_expert(pieces[k], k) for k in range(1, MOST)]
    spread = jnp.concatenate(plane, axis=0)
    spread, own_half = lax.optimization_barrier((spread, own_half))

    chunks = 2 if rows % 32 == 0 else 1
    chunk = rows // chunks
    own = [(own_half[k].astype(F32) + sent_half[k].astype(F32)).astype(BF16) for k in range(MOST)]
    got = [own[0]] + [swap_expert(own[k], k) for k in range(1, MOST)]
    masks = group_masks(experts)
    came = [swap_expert(spread, masks[-1])] if masks else []
    first = spread.shape[0]
    for mask in masks[:-1]:
        spread = jnp.concatenate([spread, swap_expert(spread, mask)], axis=0)
    spread, came, got = lax.optimization_barrier((spread, came, got))
    sums, *sends = group_sums(meta, got, chunks)
    other_sums = swap_dp(sums)
    back = []
    for c in range(chunks):
        base = c * (MOST - 1)
        back.append(
            [sums[0, c * chunk : (c + 1) * chunk]]
            + [swap_expert(sends[base + k - 1], k) for k in range(1, MOST)]
        )
    if len(masks) > 1:
        spread, sums = lax.optimization_barrier((spread, sums))
        came.append(swap_expert(spread[first:], masks[-1]))
    other_sums, back[0][1] = lax.optimization_barrier((other_sums, back[0][1]))
    came, back[0] = lax.optimization_barrier((came, back[0]))
    spread = jnp.concatenate([spread] + came, axis=0)
    before = ()
    for c in range(chunks):
        if c == chunks - 1:
            before, back[c] = lax.optimization_barrier((before, back[c]))
        mine = stacked(back[c])
        if c == chunks - 1:
            mine, spread = lax.optimization_barrier((mine, spread))
        other = swap_dp(mine)
        if c == chunks - 1:
            parts = project(spread, [sums, other_sums])
            parts, gate_rows, other = lax.optimization_barrier((parts, gate_rows, other))
        before = crossed(meta, mine, other, gate_rows, up_rows, c, chunks, before)
    gram, raw = before
    if lax.axis_size("tensor") > 1:
        gram, raw = lax.psum((gram, raw), "tensor")
        parts = [lax.psum(value.astype(F32), "tensor").astype(BF16) for value in parts]
    arrived = [parts[0]] + [swap_expert(parts[k], k) for k in range(1, MOST)]
    inverse = factored(gram)
    inverse, arrived = lax.optimization_barrier((inverse, arrived))
    coeff = coefficients(inverse, raw)
    other_coeff = swap_dp(coeff)
    shares = spread[:, :LANES]
    sides = hidden_rows(meta, inverse, coeff, other_coeff, shares, arrived, toks)
    return scattered_answers(sides, down_rows, toks)


def solution(mesh):
    return jax.shard_map(
        on_device,
        mesh=mesh,
        in_specs=(
            P(("expert", "dp"), "tensor"),
            P("expert", "tensor", "dp"),
            P("expert", "tensor", "dp"),
            P("expert", "dp", "tensor"),
            P("expert", None, "dp", None),
            P(),
            P(("expert", "dp"), None),
            P(("expert", "dp"), None),
        ),
        out_specs=P(("expert", "dp"), "tensor"),
        check_vma=False,
    )
```
